512 devices in a mesh: group: 64 (over x, y, core), tensor: 8 (over z).
Axes of the slice: x: 4, y: 8, z: 8, core: 2. Of those that a mesh axis runs over, the one named last changes fastest.
Arguments:
- tokens: bfloat16 [24576, 8192], P('group', 'tensor'), may hold values from -6 to 6
- w_key: bfloat16 [8192, 1024], P('tensor'), may hold values from -0.0625 to 0.0625
- row_adapter: int32 [24576, 1], P('group'), may hold values from 0 to 127; in each aligned block of 384 rows (0 to 383, 384 to 767, ...) at most 4 rows name the same one
- panel_a: bfloat16 [128, 8192, 64], P('group', 'tensor'), may hold values from -0.0625 to 0.0625
- up_panels: bfloat16 [128, 64, 1024], P('group'), may hold values from -0.75 to 0.75
Outputs:
- keys: bfloat16 [1024, 24576], P('tensor', 'group')
The draws below stay inside these ranges and needn't reach their ends.
Inputs may be any that keep to these rules, and one draw needn't show every extreme that they name: `row_adapter`: in the rows of one group (aligned blocks of 384 rows) no adapter is named by more than 4 rows; in every draw some group names some adapter exactly 4 times.
All inputs are finite; a program needn't handle non-finite values.
Results may differ from the reference program's by a relative error of at most 0.0095.
Values may be sent and summed in bfloat16 or wider, within the bound.
A program may use at most 64 MiB of HBM per device.

```python
import math
import jax
import jax.numpy as jnp
import numpy as np
from jax import lax

D = 8192
KV = 1024
RANK = 64
ROWS = 384
ADAPTER_TOTAL = 128
CAP = 4
ROWS_ALL = 24576
N_GROUP = 64


def block_levels(key, dims, split, low, largest):
    def one(axis_at, shards_of):
        steps = jax.random.uniform(jax.random.fold_in(jax.random.fold_in(key, 6), axis_at), (shards_of,), jnp.float32, low / len(split), largest / len(split))
        return jnp.repeat(jnp.exp(steps), dims[axis_at] // shards_of).reshape((-1,) + (1,) * (len(dims) - axis_at - 1))

    loudness = one(*split[0])
    for cut in split[1:]:
        loudness = loudness * one(*cut)
    return loudness


def assign_block(key, own, number, rows, count, top, limit, lean):
    sequence = jax.random.permutation(key, count)
    packed, common = load_shares(count, rows * top, limit, lean, True), load_shares(count, rows * top, limit, lean, False)
    places = jnp.arange(count)

    def named(lengths, offset_by):
        used = int((lengths > 0).sum())
        fixed = max(1, used // 4)
        moved = fixed + (places - fixed + offset_by * (used - fixed)) % max(1, count - fixed)
        return jnp.zeros((count,), jnp.int32).at[sequence[jnp.where(places < fixed, places, moved)]].set(jnp.asarray(lengths, jnp.int32))

    lengths = jnp.where(number % 4 == 0, named(packed, number // 4), named(common, number - number // 4 - 1))
    mixed = jax.random.permutation(jax.random.fold_in(own, 3), count)
    giver, receiver = mixed[0:count // 2 * 2:2], mixed[1:count // 2 * 2:2]
    slack = jnp.minimum(lengths[giver] - 1, limit - lengths[receiver]) // 2
    slack = jnp.where((giver == sequence[0]) | (receiver == sequence[0]) | (lengths[receiver] == 0), 0, jnp.maximum(slack, 0))
    moved = jax.random.randint(jax.random.fold_in(own, 4), (count // 2,), 0, 1 << 20) % (slack + 1)
    lengths = lengths.at[giver].add(-moved).at[receiver].add(moved)
    members = jnp.searchsorted(jnp.cumsum(lengths), jnp.arange(rows * top), side="right").astype(jnp.int32)
    table = members.reshape(top, rows).T
    table = table[jax.random.permutation(jax.random.fold_in(own, 1), rows)]
    offset_by = jax.random.randint(jax.random.fold_in(own, 2), (rows, 1), 0, top)
    return jnp.take_along_axis(table, (jnp.arange(top)[None, :] + offset_by) % top, axis=1)


def load_shares(amount, total, bound, slope, full):
    weights = [(1 << 20) // math.isqrt(grade ** slope) + 1 for grade in range(1, amount + 1)]
    largest = bound if full else min(bound, max(-(-total // amount), total * weights[0] // sum(weights)))
    least = 1 if total - largest >= amount - 1 else 0
    given, spare = [largest] + [least] * (amount - 1), total - largest - least * (amount - 1)
    while spare > 0:
        candidates = [i for i in range(1, amount) if given[i] < largest] or [i for i in range(1, amount) if given[i] < bound]
        whole, remaining = sum([weights[i] for i in candidates]), spare
        for i in candidates:
            extra = min(bound - given[i], max(1, remaining * weights[i] // whole), spare)
            given[i] = given[i] + extra
            spare = spare - extra
    return np.array(given)


def noise(stream_key, dims, spread, limit, cuts=(), kind=jnp.bfloat16):
    result = spread * jax.random.normal(stream_key, dims, jnp.float32)
    if cuts:
        result = result * block_levels(stream_key, dims, cuts, -0.22, 0.18)
    return jnp.clip(result, -limit, limit).astype(kind)


def setup_inputs(seed: int = 0) -> dict:
    splits = jax.random.split(jax.random.key(seed), 6)
    tokens = noise(splits[0], (ROWS_ALL, D), 1.0, 6.0, ((0, 64), (1, 8)))
    w_key = noise(splits[1], (D, KV), D ** -0.5, 0.0625, ((0, 8),))
    row_adapter_keys = jax.random.split(jax.random.fold_in(splits[2], 1), ROWS_ALL // ROWS)
    row_adapter_turns = jax.random.permutation(jax.random.fold_in(splits[2], 3), ROWS_ALL // ROWS)
    row_adapter = jax.vmap(lambda own, number: assign_block(jax.random.fold_in(splits[2], 2), own, number, ROWS, ADAPTER_TOTAL, 1, CAP, 2))(row_adapter_keys, row_adapter_turns).reshape((ROWS_ALL, 1))
    panel_a = noise(splits[3], (ADAPTER_TOTAL, D, RANK), D ** -0.5, 0.0625, ((0, 64), (1, 8)))
    up_panels = noise(splits[4], (ADAPTER_TOTAL, RANK, KV), RANK ** -0.5, 0.75, ((0, 64),))
    return {"tokens": tokens, "w_key": w_key, "row_adapter": row_adapter, "panel_a": panel_a, "up_panels": up_panels}


def reference(tokens, w_key, row_adapter, panel_a, up_panels):
    adapter_ids = row_adapter[:, 0].astype(jnp.int32)
    row_combined = adapter_ids.shape[0]
    base_projection = jnp.dot(tokens, w_key, preferred_element_type=jnp.float32)
    sorted_rows = jnp.argsort(adapter_ids, stable=True).astype(jnp.int32)
    counts = jnp.bincount(adapter_ids, length=ADAPTER_TOTAL).astype(jnp.int32)
    starts = (jnp.cumsum(counts) - counts).astype(jnp.int32)
    longest = N_GROUP * CAP
    padded = jnp.concatenate([sorted_rows, jnp.full((longest,), row_combined, jnp.int32)])

    def adapter_grouped(adapter_choice):
        selected_rows = lax.dynamic_slice(padded, (starts[adapter_choice],), (longest,))
        valid_mask = jnp.arange(longest, dtype=jnp.int32) < counts[adapter_choice]
        selected_rows = jnp.where(valid_mask, selected_rows, row_combined).astype(jnp.int32)
        picked = tokens[jnp.minimum(selected_rows, row_combined - 1)]
        rank_vector = jnp.dot(picked, panel_a[adapter_choice], preferred_element_type=jnp.float32)
        lowrank_delta = jnp.dot(rank_vector, up_panels[adapter_choice].astype(jnp.float32), precision=lax.Precision.HIGHEST)
        return selected_rows, jnp.where(valid_mask[:, None], lowrank_delta, jnp.float32(0.0))

    every_request_row, every_lowrank_output = lax.map(adapter_grouped, jnp.arange(ADAPTER_TOTAL, dtype=jnp.int32))
    adapter_delta = jnp.zeros((row_combined + 1, base_projection.shape[1]), jnp.float32)
    adapter_delta = adapter_delta.at[every_request_row.reshape(-1)].add(every_lowrank_output.reshape(-1, base_projection.shape[1]))[:row_combined]
    return (base_projection + adapter_delta).T.astype(jnp.bfloat16)
```

```python
import functools

import jax
import jax.numpy as jnp
from jax import lax
from jax.experimental import pallas as pl
from jax.experimental.pallas import tpu as pltpu
from jax.sharding import PartitionSpec as P

MESH = pl.DeviceIdType.MESH
F32, BF16 = jnp.float32, jnp.bfloat16
X, Y = 4, 8
CAP = 4


def kernel(dims, ids_ref, tok_hbm, w_hbm, pa_hbm, up_hbm, out_ref,
           tok, w, pa, up, place, send, recv, bsend, brecv, base, rsend, rrecv, lsend, lrecv,
           in_sem, tok_ss, tok_rs, b_ss, b_rs, r_ss, r_rs, l_ss, l_rs):
    nx, ny, nz = dims
    nxc = 2 * nx
    ng = nxc * ny
    sets = ng // nz
    rows, width = tok.shape
    half = width // 2
    feat, keys = out_ref.shape[0], w.shape[1]
    slots = 2 * CAP
    self_at = ((nxc - ny % nxc) % nxc) * ny + ny - 1

    me, t = lax.axis_index("group"), lax.axis_index("tensor")
    mc, my, mx = lax.rem(me, 2), lax.rem(lax.div(me, 2), ny), lax.div(me, 2 * ny)

    def offsets(i):
        k, m = lax.div(i, ny), lax.rem(i, ny)
        h = lax.div(m, 2)
        odd = lax.rem(m, 2)
        dy = odd * (ny // 2 - 1 - h) + (1 - odd) * (ny // 2 + h)
        q = lax.rem(k + m + 1, nxc)
        return lax.div(q, 2), dy, lax.rem(q, 2)

    def dest(i):
        dx, dy, dc = offsets(i)
        return (lax.rem(mx + dx, nx) * ny + lax.rem(my + dy, ny)) * 2 + lax.rem(mc + dc, 2)

    def source(i):
        dx, dy, dc = offsets(i)
        return (lax.rem(mx - dx + nx, nx) * ny + lax.rem(my - dy + ny, ny)) * 2 + lax.rem(mc + dc, 2)

    loads = [pltpu.make_async_copy(a, b, in_sem.at[n])
             for n, (a, b) in enumerate(((tok_hbm, tok), (w_hbm, w), (pa_hbm, pa), (up_hbm, up)))]
    for c in loads:
        c.start()

    barrier = pltpu.get_barrier_semaphore()

    @pl.loop(0, ng)
    def _(i):
        @pl.when(i != self_at)
        def _():
            pl.semaphore_signal(barrier, inc=1, device_id={"group": dest(i)}, device_id_type=MESH)

    @pl.loop(1, nz)
    def _(j):
        pl.semaphore_signal(barrier, inc=1, device_id={"tensor": lax.rem(t + j, nz)}, device_id_type=MESH)

    ids = ids_ref[...]
    one_hot = (lax.broadcasted_iota(jnp.int32, (2 * ng, rows), 0) == ids).astype(F32)
    earlier = (lax.broadcasted_iota(jnp.int32, (rows, rows), 0)
               < lax.broadcasted_iota(jnp.int32, (rows, rows), 1)).astype(F32).astype(BF16)
    before = jnp.dot(one_hot.astype(BF16), earlier, preferred_element_type=F32)
    rank = jnp.sum(before * one_hot, axis=0, keepdims=True)
    slot = ids.astype(F32) * CAP + rank
    total = ng * slots
    part = min(128, total)
    loads[0].wait()
    for c in range(total // part):
        at = lax.broadcasted_iota(jnp.int32, (part, rows), 0).astype(F32) + float(c * part)
        chosen = (at == slot).astype(F32).astype(BF16)
        place[c * part:(c + 1) * part, :] = chosen
        g = jnp.dot(chosen, tok[...], preferred_element_type=F32)
        n = part // slots
        both = jnp.concatenate([g[:, :half].reshape(n, slots, half), g[:, half:].reshape(n, slots, half)], axis=1)
        send[c * n:(c + 1) * n] = both.astype(BF16)

    pl.semaphore_wait(barrier, ng - 1 + nz - 1)

    def token_copy(i, n=1):
        d = dest(i)
        return pltpu.make_async_remote_copy(
            send.at[d], recv.at[i], tok_ss, tok_rs.at[i], device_id={"group": d}, device_id_type=MESH)

    @pl.loop(0, ng)
    def _(i):
        @pl.when(i != self_at)
        def _():
            token_copy(i).start()

    recv[self_at] = send[me]

    def base_part(peer):
        block = w[:, pl.ds(pl.multiple_of(peer * feat, feat), feat)]
        return lax.dot_general(block, tok[...], (((0,), (1,)), ((), ())), preferred_element_type=F32)

    def base_copy(j):
        return pltpu.make_async_remote_copy(
            bsend.at[j], brecv.at[j], b_ss.at[j], b_rs.at[j],
            device_id={"tensor": lax.rem(t + j, nz)}, device_id_type=MESH)

    loads[1].wait()

    @pl.loop(0, nz - 1)
    def _(n):
        h, odd = lax.div(n, 2), lax.rem(n, 2)
        j = odd * (nz // 2 - 1 - h) + (1 - odd) * (nz // 2 + h)
        bsend[j] = base_part(lax.rem(t + j, nz)).astype(BF16)
        base_copy(j).start()

    base[...] = base_part(t)

    loads[2].wait()
    loads[3].wait()
    panel = jnp.concatenate([pa[0, :, :half], pa[1, :, :half], pa[0, :, half:], pa[1, :, half:]], axis=0)
    rk = pa.shape[1]
    ups = jnp.concatenate([up[0], up[1], up[0], up[1]], axis=0)

    def rank_copy(k):
        return pltpu.make_async_remote_copy(
            rsend.at[k], rrecv.at[t], r_ss.at[k], r_rs.at[t], device_id={"tensor": k}, device_id_type=MESH)

    def rank_from(p):
        return pltpu.make_async_remote_copy(
            rsend.at[p], rrecv.at[p], r_ss.at[p], r_rs.at[p], device_id={"tensor": p}, device_id_type=MESH)

    def swap(v):
        return jnp.concatenate([v[:, CAP:], v[:, :CAP]], axis=1)

    pair_shape = (sets // 2, slots, 2 * rk)
    top = lax.broadcasted_iota(jnp.int32, pair_shape, 1) < CAP
    first = lax.broadcasted_iota(jnp.int32, pair_shape, 2) < rk

    def lora_copy(n):
        s, p = lax.div(n, nz), lax.rem(n, nz)
        return pltpu.make_async_remote_copy(
            lsend.at[s, p], lrecv.at[me], l_ss.at[n], l_rs.at[me],
            device_id={"group": source(t * sets + s), "tensor": p}, device_id_type=MESH)

    def lora_stays(n):
        return (t * sets + lax.div(n, nz) == self_at) & (lax.rem(n, nz) == t)

    @pl.loop(0, nz + 1)
    def _(k):
        @pl.when(k < nz)
        def _():
            @pl.loop(0, sets)
            def _(s):
                i = k * sets + s

                @pl.when(i != self_at)
                def _():
                    token_copy(i).wait_recv()

            x = recv[pl.ds(k * sets, sets)].reshape(sets * 2 * slots, half)
            r = lax.dot_general(x, panel, (((1,), (1,)), ((), ())), preferred_element_type=F32)
            r = r.reshape(sets, 2 * slots, 4 * rk)
            v = (r[:, :slots, :2 * rk] + r[:, slots:, 2 * rk:]).reshape(sets // 2, 2, slots, 2 * rk)
            even, odd = v[:, 0], v[:, 1]
            packed = jnp.where(top, jnp.where(first, even, swap(even)), jnp.where(first, swap(odd), odd))

            @pl.when(k != t)
            def _():
                rsend[k] = packed
                rank_copy(k).start()

            @pl.when(k == t)
            def _():
                rrecv[k] = packed

        @pl.when(k == t + 1)
        def _():
            @pl.loop(1, nz)
            def _(j):
                rank_from(lax.rem(t + j, nz)).wait_recv()

            v = rrecv[0]
            for p in range(1, nz):
                v = v + rrecv[p]
            zero = jnp.zeros_like(v)
            other = swap(v)
            even = jnp.where(top, jnp.where(first, v, zero), jnp.where(first, zero, other))
            odd = jnp.where(top, jnp.where(first, other, zero), jnp.where(first, zero, v))
            lhs = jnp.concatenate([even[:, None], odd[:, None]], axis=1).reshape(sets * slots, 2 * rk)
            high = lhs.astype(BF16)
            low = (lhs - high.astype(F32)).astype(BF16)
            lora = jnp.dot(jnp.concatenate([high, low], axis=1), ups, preferred_element_type=F32)
            for p in range(nz):
                lsend[:, p] = lora[:, p * feat:(p + 1) * feat].reshape(sets, slots, feat).astype(BF16)

            @pl.loop(0, sets * nz)
            def _(n):
                @pl.when(jnp.logical_not(lora_stays(n)))
                def _():
                    lora_copy(n).start()

            @pl.when(t == self_at // sets)
            def _():
                lrecv[me] = lsend[self_at % sets, t]

    @pl.loop(1, nz)
    def _(j):
        base_copy(j).wait_recv()

    acc = base[...]
    for j in range(1, nz):
        acc = acc + brecv[j].astype(F32)

    @pl.loop(0, ng)
    def _(g):
        @pl.when(jnp.logical_not((g == me) & (t == self_at // sets)))
        def _():
            pltpu.make_async_remote_copy(
                lsend.at[0, 0], lrecv.at[g], l_ss.at[0], l_rs.at[g],
                device_id={"group": g}, device_id_type=MESH).wait_recv()

    back = lrecv[...].astype(F32).reshape(total, feat).astype(BF16)
    acc = acc + lax.dot_general(back, place[...], (((0,), (0,)), ((), ())), preferred_element_type=F32)
    out_ref[...] = acc.astype(BF16)

    pltpu.make_async_remote_copy(
        send.at[pl.ds(0, ng - 1)], recv.at[pl.ds(0, ng - 1)], tok_ss, tok_rs.at[0],
        device_id={"group": me}, device_id_type=MESH).wait_send()

    @pl.loop(1, nz)
    def _(j):
        base_copy(j).wait_send()
        rank_copy(lax.rem(t + j, nz)).wait_send()

    @pl.loop(0, sets * nz)
    def _(n):
        @pl.when(jnp.logical_not(lora_stays(n)))
        def _():
            lora_copy(n).wait_send()


def local(dims, tokens, w_key, row_adapter, panel_a, up_panels):
    nx, ny, nz = dims
    ng = 2 * nx * ny
    rows, width = tokens.shape
    keys = w_key.shape[1]
    feat = keys // nz
    sets = ng // nz
    rk = panel_a.shape[2]
    vmem = pl.BlockSpec(memory_space=pltpu.VMEM)
    hbm = pl.BlockSpec(memory_space=pl.ANY)
    dma = pltpu.SemaphoreType.DMA
    return pl.pallas_call(
        functools.partial(kernel, dims),
        out_shape=jax.ShapeDtypeStruct((feat, rows), BF16),
        in_specs=[vmem, hbm, hbm, hbm, hbm],
        out_specs=vmem,
        scratch_shapes=[
            pltpu.VMEM((rows, width), BF16),
            pltpu.VMEM(w_key.shape, BF16),
            pltpu.VMEM((2, rk, width), BF16),
            pltpu.VMEM(up_panels.shape, BF16),
            pltpu.VMEM((2 * CAP * ng, rows), BF16),
            pltpu.VMEM((ng, 4 * CAP, width // 2), BF16),
            pltpu.VMEM((ng, 4 * CAP, width // 2), BF16),
            pltpu.VMEM((nz, feat, rows), BF16),
            pltpu.VMEM((nz, feat, rows), BF16),
            pltpu.VMEM((feat, rows), F32),
            pltpu.VMEM((nz, sets // 2, 2 * CAP, 2 * rk), F32),
            pltpu.VMEM((nz, sets // 2, 2 * CAP, 2 * rk), F32),
            pltpu.VMEM((sets, nz, 2 * CAP, feat), BF16),
            pltpu.VMEM((ng, 2 * CAP, feat), BF16),
            dma((4,)),
            dma,
            dma((ng,)),
            dma((nz,)),
            dma((nz,)),
            dma((nz,)),
            dma((nz,)),
            dma((sets * nz,)),
            dma((ng,)),
        ],
        compiler_params=pltpu.CompilerParams(
            collective_id=0, has_side_effects=True, vmem_limit_bytes=48 * 1024 * 1024),
    )(row_adapter.reshape(1, rows), tokens, w_key, jnp.swapaxes(panel_a, 1, 2), up_panels)


def solution(mesh):
    return jax.shard_map(
        functools.partial(local, (X, Y, mesh.shape["tensor"])),
        mesh=mesh,
        in_specs=(
            P("group", "tensor"),
            P("tensor", None),
            P("group", None),
            P("group", "tensor", None),
            P("group", None, None),
        ),
        out_specs=P("tensor", "group"),
        check_vma=False,
    )
```

```python
import functools

import jax
import jax.numpy as jnp
from jax import lax
from jax.experimental import pallas as pl
from jax.experimental.pallas import tpu as pltpu
from jax.sharding import PartitionSpec as P

MESH = pl.DeviceIdType.MESH
F32, BF16 = jnp.float32, jnp.bfloat16
X, Y = 4, 8
CAP = 4
BATCHES = 2


def kernel(dims, ids_ref, tok_hbm, w_hbm, pa_hbm, up_hbm, out_ref,
           tok, w, panels, place, send, recv, part, zs, zr, rsend, rrecv, full, lsend, lrecv,
           in_sem, y_ss, y_rs, x_ss, x_rs, z_ss, z_rs, r_ss, r_rs, a_ss, a_rs, l_ss, l_rs):
    nx, ny, nz = dims
    nq = 2 * nx
    half, hz = ny // 2, nz // 2
    nb = half // BATCHES
    rows, width = tok.shape
    feat = out_ref.shape[0]
    rk = panels.shape[2]
    span = nb * 4 * CAP

    me, t = lax.axis_index("group"), lax.axis_index("tensor")
    mc, my, mx = lax.rem(me, 2), lax.rem(lax.div(me, 2), ny), lax.div(me, 2 * ny)
    mq = mx * 2 + mc

    def along_x(q):
        return {"group": (lax.div(q, 2) * ny + my) * 2 + lax.rem(q, 2)}

    def along_y(step):
        return {"group": (mx * ny + lax.rem(my + step + ny, ny)) * 2 + mc}

    def along_z(p):
        return {"tensor": p}

    def remote(src, dst, ss, rs, where):
        return pltpu.make_async_remote_copy(src, dst, ss, rs, device_id=where, device_id_type=MESH)

    mine = pl.ds(pl.multiple_of(t * feat, feat), feat)
    loads = [
        pltpu.make_async_copy(pa_hbm, panels.at[0, :, :, pl.ds(0, width)], in_sem.at[0]),
        pltpu.make_async_copy(up_hbm.at[:, :, mine], panels.at[0, :, :, pl.ds(width, feat)], in_sem.at[1]),
        pltpu.make_async_copy(tok_hbm, tok, in_sem.at[2]),
        pltpu.make_async_copy(w_hbm, w, in_sem.at[3]),
    ]
    for c in loads:
        c.start()

    barrier = pltpu.get_barrier_semaphore()
    for step in (-1, 1):
        pl.semaphore_signal(barrier, inc=1, device_id=along_y(step), device_id_type=MESH)

    @pl.loop(1, nz)
    def _(j):
        pl.semaphore_signal(barrier, inc=1, device_id=along_z(lax.rem(t + j, nz)), device_id_type=MESH)

    @pl.loop(1, nq)
    def _(j):
        pl.semaphore_signal(barrier, inc=1, device_id=along_x(lax.rem(mq + j, nq)), device_id_type=MESH)

    ids = ids_ref[...]
    one_hot = (lax.broadcasted_iota(jnp.int32, (2 * nq * ny, rows), 0) == ids).astype(F32)
    earlier = (lax.broadcasted_iota(jnp.int32, (rows, rows), 0)
               < lax.broadcasted_iota(jnp.int32, (rows, rows), 1)).astype(F32).astype(BF16)
    before = jnp.dot(one_hot.astype(BF16), earlier, preferred_element_type=F32)
    rank = jnp.sum(before * one_hot, axis=0, keepdims=True)
    second, core = lax.rem(ids, 2), lax.rem(lax.div(ids, 2), 2)
    home_y, home_x = lax.rem(lax.div(ids, 4), ny), lax.div(ids, 4 * ny)
    off = lax.rem(home_y - my + ny, ny)
    last = (off == 0) | (off == half)
    pair = jnp.where(last, half - 1, jnp.where(off < half, off - 1, ny - 1 - off))
    side = jnp.where(off < half, 0, 1)
    at = (lax.div(pair, nb) * nq + home_x * 2 + core) * span
    at = at + (lax.rem(pair, nb) * 2 + side) * 2 * CAP + second * CAP
    slot = at.astype(F32) + rank
    total = BATCHES * nq * span
    place[...] = (lax.broadcasted_iota(jnp.int32, (total, rows), 0).astype(F32) == slot).astype(F32).astype(BF16)

    pl.semaphore_wait(barrier, nq + nz)

    below = [(d, j) for d in range(1, half) for j in (0, 1)] + [(half, 0)]
    above = [(d, 1 - j) for d, j in below]

    def y_copy(n, way):
        d, j = (below if way > 0 else above)[n]
        src, dst = (-(d - 1) * way) % ny, (-d * way) % ny
        return remote(panels.at[src, j], panels.at[dst, j], y_ss.at[n, (1 - way) // 2], y_rs.at[n, (1 - way) // 2],
                      along_y(way))

    loads[0].wait()
    loads[1].wait()
    order = [(d, j) for d, j in below]

    def y_start(n):
        y_copy(n, 1).start()
        y_copy(n, -1).start()

    def y_step(n):
        y_copy(n, 1).wait_recv()
        y_copy(n, -1).wait_recv()
        if n + 2 < len(order):
            y_start(n + 2)
        elif n + 2 == len(order):
            pass

    y_start(0)
    y_start(1)

    loads[2].wait()
    cols = min(256, width)
    for c in range(width // cols):
        g = jnp.dot(place[...], tok[:, c * cols:(c + 1) * cols], preferred_element_type=F32)
        send[:, :, :, c * cols:(c + 1) * cols] = g.reshape(BATCHES, nq, span, cols).astype(BF16)

    def x_copy(n, at_q, q):
        b = lax.div(n, nq - 1)
        return remote(send.at[b, q], recv.at[b, at_q], x_ss.at[n], x_rs.at[n], along_x(q))

    @pl.loop(0, BATCHES * (nq - 1))
    def _(n):
        x_copy(n, mq, lax.rem(mq + lax.rem(n, nq - 1) + 1, nq)).start()

    for b in range(BATCHES):
        recv[b, mq] = send[b, mq]

    loads[3].wait()
    for c in range(nz // 2):
        g = jnp.dot(tok[...], w[:, c * 2 * feat:(c + 1) * 2 * feat], preferred_element_type=F32)
        part[2 * c] = g[:, :feat]
        part[2 * c + 1] = g[:, feat:]

    def z_copy(s, way):
        k = (1 - way) // 2
        return remote(zs.at[k, s], zr.at[k, s], z_ss.at[k, s], z_rs.at[k, s], along_z(lax.rem(t + way + nz, nz)))

    def z_step(s):
        for way, hops in ((1, hz), (-1, hz - 1)):
            if s >= hops:
                continue
            k = (1 - way) // 2
            v = part[lax.rem(t + way * (hops - s) + nz, nz)]
            if s > 0:
                z_copy(s - 1, way).wait_recv()
                v = v + zr[k, s - 1].astype(F32)
            zs[k, s] = v.astype(BF16)
            z_copy(s, way).start()

    top = lax.broadcasted_iota(jnp.int32, (nx, 2 * CAP, 2 * rk), 1) < CAP
    first = lax.broadcasted_iota(jnp.int32, (nx, 2 * CAP, 2 * rk), 2) < rk

    def swap(v):
        return jnp.concatenate([v[:, CAP:], v[:, :CAP]], axis=1)

    def offsets(m):
        return (0, half) if m == half - 1 else (m + 1, ny - 1 - m)

    def x_wait(b):
        @pl.loop(0, nq - 1)
        def _(n):
            x_copy(b * (nq - 1) + n, mq, mq).wait_recv()

    def rank_part(b, mm):
        e0, e1 = offsets(b * nb + mm)
        down = jnp.concatenate([panels[e, j, :, :width] for e in (e0, e1) for j in (0, 1)], axis=0)
        x = recv[b, :, mm * 4 * CAP:(mm + 1) * 4 * CAP, :].reshape(nq * 4 * CAP, width)
        r = lax.dot_general(x, down, (((1,), (1,)), ((), ())), preferred_element_type=F32)
        r = r.reshape(nq, 4 * CAP, 4 * rk)
        for e in (0, 1):
            v = r[:, e * 2 * CAP:(e + 1) * 2 * CAP, e * 2 * rk:(e + 1) * 2 * rk].reshape(nx, 2, 2 * CAP, 2 * rk)
            even, odd = v[:, 0], v[:, 1]
            packed = jnp.where(top, jnp.where(first, even, swap(even)), jnp.where(first, swap(odd), odd))
            for i in range(nx):
                rsend[b, 2 * i + e, mm] = packed[i]

    def sum_copy(b, p, at_p):
        return remote(rsend.at[b, p], rrecv.at[b, at_p], r_ss.at[b, p], r_rs.at[b, at_p], along_z(p))

    def sum_start(b):
        @pl.loop(1, nz)
        def _(j):
            sum_copy(b, lax.rem(t + j, nz), t).start()

        rrecv[b, t] = rsend[b, t]

    def full_copy(b, p, at_p):
        return remote(full.at[b, at_p], full.at[b, at_p], a_ss.at[b, p], a_rs.at[b, at_p], along_z(p))

    def full_start(b):
        @pl.loop(1, nz)
        def _(j):
            p = lax.rem(t + j, nz)
            sum_copy(b, p, p).wait_recv()

        v = rrecv[b, 0]
        for p in range(1, nz):
            v = v + rrecv[b, p]
        full[b, t] = v

        @pl.loop(1, nz)
        def _(j):
            full_copy(b, lax.rem(t + j, nz), t).start()

    def lora_copy(b, q, at_q):
        return remote(lsend.at[b, q], lrecv.at[b, at_q], l_ss.at[b, q], l_rs.at[b, at_q], along_x(q))

    def lora_start(b):
        @pl.loop(1, nz)
        def _(j):
            p = lax.rem(t + j, nz)
            full_copy(b, p, p).wait_recv()

        tiles = full[b].reshape(nx, 2, nb, 2 * CAP, 2 * rk)
        zero = jnp.zeros((nx, 2 * CAP, 2 * rk), F32)
        for mm in range(nb):
            for side_at, e in enumerate(offsets(b * nb + mm)):
                v = tiles[:, side_at, mm]
                other = swap(v)
                even = jnp.where(top, jnp.where(first, v, zero), jnp.where(first, zero, other))
                odd = jnp.where(top, jnp.where(first, other, zero), jnp.where(first, zero, v))
                lhs = jnp.concatenate([even[:, None], odd[:, None]], axis=1).reshape(nq * 2 * CAP, 2 * rk)
                high = lhs.astype(BF16)
                low = (lhs - high.astype(F32)).astype(BF16)
                ups = jnp.concatenate([panels[e, j, :, width:] for j in (0, 1)] * 2, axis=0)
                g = jnp.dot(jnp.concatenate([high, low], axis=1), ups, preferred_element_type=F32)
                g = g.reshape(nq, 2 * CAP, feat)
                if side_at == 0:
                    kept = g
                else:
                    lsend[b, :, mm * 4 * CAP:(mm + 1) * 4 * CAP, :] = jnp.concatenate([kept, g], axis=1).astype(BF16)

        @pl.loop(1, nq)
        def _(j):
            lora_copy(b, lax.rem(mq + j, nq), mq).start()

        lrecv[b, mq] = lsend[b, mq]

    def lora_add(b):
        @pl.loop(1, nq)
        def _(j):
            q = lax.rem(mq + j, nq)
            lora_copy(b, q, q).wait_recv()

        back = lrecv[b].reshape(nq * span, feat)
        return lax.dot_general(back, place[b * nq * span:(b + 1) * nq * span, :], (((0,), (0,)), ((), ())),
                               preferred_element_type=F32)

    ready = [2 * nb * (b + 1) - 1 for b in range(BATCHES - 1)] + [len(order) - 1]
    for n in range(ready[0] + 1):
        if n < hz:
            z_step(n)
        y_step(n)
    x_wait(0)
    for mm in range(nb):
        rank_part(0, mm)
    sum_start(0)
    x_wait(1)
    for n in range(ready[0] + 1, len(order) - 1):
        y_step(n)
    for s in range(ready[0] + 1, hz):
        z_step(s)
    full_start(0)
    for mm in range(nb - 1):
        rank_part(1, mm)
    acc = part[t]
    for way, hops in ((1, hz), (-1, hz - 1)):
        z_copy(hops - 1, way).wait_recv()
        acc = acc + zr[(1 - way) // 2, hops - 1].astype(F32)
    acc = acc.T
    lora_start(0)
    y_step(len(order) - 1)
    rank_part(1, nb - 1)
    sum_start(1)
    acc = acc + lora_add(0)
    full_start(1)
    lora_start(1)
    out_ref[...] = (acc + lora_add(1)).astype(BF16)

    for n in range(len(order)):
        y_copy(n, 1).wait_send()
        y_copy(n, -1).wait_send()

    @pl.loop(0, BATCHES * (nq - 1))
    def _(n):
        x_copy(n, mq, mq).wait_send()

    for way, hops in ((1, hz), (-1, hz - 1)):
        for s in range(hops):
            z_copy(s, way).wait_send()
    for b in range(BATCHES):
        @pl.loop(1, nz)
        def _(j):
            p = lax.rem(t + j, nz)
            sum_copy(b, p, t).wait_send()
            full_copy(b, p, t).wait_send()

        @pl.loop(1, nq)
        def _(j):
            lora_copy(b, lax.rem(mq + j, nq), mq).wait_send()


def local(dims, tokens, w_key, row_adapter, panel_a, up_panels):
    nx, ny, nz = dims
    rows, width = tokens.shape
    feat = w_key.shape[1] // nz
    rk = panel_a.shape[2]
    nq, half, hz = 2 * nx, ny // 2, nz // 2
    nb = half // BATCHES
    span = nb * 4 * CAP
    vmem = pl.BlockSpec(memory_space=pltpu.VMEM)
    hbm = pl.BlockSpec(memory_space=pl.ANY)
    dma = pltpu.SemaphoreType.DMA
    tiles = (BATCHES, nz, nb, 2 * CAP, 2 * rk)
    return pl.pallas_call(
        functools.partial(kernel, dims),
        out_shape=jax.ShapeDtypeStruct((feat, rows), BF16),
        in_specs=[vmem, hbm, hbm, hbm, hbm],
        out_specs=vmem,
        scratch_shapes=[
            pltpu.VMEM((rows, width), BF16),
            pltpu.VMEM(w_key.shape, BF16),
            pltpu.VMEM((ny, 2, rk, width + feat), BF16),
            pltpu.VMEM((BATCHES * nq * span, rows), BF16),
            pltpu.VMEM((BATCHES, nq, span, width), BF16),
            pltpu.VMEM((BATCHES, nq, span, width), BF16),
            pltpu.VMEM((nz, rows, feat), F32),
            pltpu.VMEM((2, hz, rows, feat), BF16),
            pltpu.VMEM((2, hz, rows, feat), BF16),
            pltpu.VMEM(tiles, F32),
            pltpu.VMEM(tiles, F32),
            pltpu.VMEM(tiles, F32),
            pltpu.VMEM((BATCHES, nq, span, feat), BF16),
            pltpu.VMEM((BATCHES, nq, span, feat), BF16),
            dma((4,)),
            dma((ny - 1, 2)),
            dma((ny - 1, 2)),
            dma((BATCHES * (nq - 1),)),
            dma((BATCHES * (nq - 1),)),
            dma((2, hz)),
            dma((2, hz)),
            dma((BATCHES, nz)),
            dma((BATCHES, nz)),
            dma((BATCHES, nz)),
            dma((BATCHES, nz)),
            dma((BATCHES, nq)),
            dma((BATCHES, nq)),
        ],
        compiler_params=pltpu.CompilerParams(
            collective_id=0, has_side_effects=True, vmem_limit_bytes=62 * 1024 * 1024),
    )(row_adapter.reshape(1, rows), tokens, w_key, jnp.swapaxes(panel_a, 1, 2), up_panels)


def solution(mesh):
    return jax.shard_map(
        functools.partial(local, (X, Y, mesh.shape["tensor"])),
        mesh=mesh,
        in_specs=(
            P("group", "tensor"),
            P("tensor", None),
            P("group", None),
            P("group", "tensor", None),
            P("group", None, None),
        ),
        out_specs=P("tensor", "group"),
        check_vma=False,
    )
```

```python
import functools

import jax
import jax.numpy as jnp
from jax import lax
from jax.experimental import pallas as pl
from jax.experimental.pallas import tpu as pltpu
from jax.sharding import PartitionSpec as P

MESH = pl.DeviceIdType.MESH
F32, BF16 = jnp.float32, jnp.bfloat16
X, Y = 4, 8
CAP = 4

def batches(ny):
    half = ny // 2
    over_z = [[0, 1, ny - 1]] + [[d, ny - d] for d in range(2, half)] + [[half]]
    early = [e for d in range(1, half - 1) for e in (d, ny - d)]
    back = ([early] if early else []) + [[half - 1, half + 1], [0, half]]
    return over_z, back


def kernel(dims, ids_ref, tok_hbm, w_hbm, pa_hbm, up_hbm, out_ref,
           tok, w, panels, place, send, recv, part, zs, zr, rsend, rrecv, rown, widened, lsend, lrecv,
           in_sem, y_ss, y_rs, x_ss, x_rs, z_ss, z_rs, r_ss, r_rs, l_ss, l_rs):
    nx, ny, nz = dims
    nq = 2 * nx
    half, hz = ny // 2, nz // 2
    rows, width = tok.shape
    feat = out_ref.shape[0]
    rk = panels.shape[2]
    slots = 2 * CAP
    over_z, back = batches(ny)
    order = [e for b in over_z for e in b]
    begin, where_back = [], {}
    for b, offs in enumerate(back):
        begin.append(sum(len(o) for o in back[:b]) * nq * slots)
        for i, e in enumerate(offs):
            where_back[e] = (b, i)

    me, t = lax.axis_index("group"), lax.axis_index("tensor")
    mc, my, mx = lax.rem(me, 2), lax.rem(lax.div(me, 2), ny), lax.div(me, 2 * ny)
    mq = mx * 2 + mc

    def along_x(q):
        return {"group": (lax.div(q, 2) * ny + my) * 2 + lax.rem(q, 2)}

    def along_y(step):
        return {"group": (mx * ny + lax.rem(my + step + ny, ny)) * 2 + mc}

    def along_z(p):
        return {"tensor": p}

    def remote(src, dst, ss, rs, where):
        return pltpu.make_async_remote_copy(src, dst, ss, rs, device_id=where, device_id_type=MESH)

    barrier = pltpu.get_barrier_semaphore()
    for step in (-1, 1):
        pl.semaphore_signal(barrier, inc=1, device_id=along_y(step), device_id_type=MESH)

    mine = pl.ds(pl.multiple_of(t * feat, feat), feat)
    loads = [
        pltpu.make_async_copy(pa_hbm, panels.at[0, :, :, pl.ds(0, width)], in_sem.at[0]),
        pltpu.make_async_copy(up_hbm.at[:, :, mine], panels.at[0, :, :, pl.ds(width, feat)], in_sem.at[1]),
        pltpu.make_async_copy(tok_hbm, tok, in_sem.at[2]),
        pltpu.make_async_copy(w_hbm, w, in_sem.at[3]),
    ]
    for c in loads:
        c.start()

    @pl.loop(1, nq)
    def _(j):
        pl.semaphore_signal(barrier, inc=1, device_id=along_x(lax.rem(mq + j, nq)), device_id_type=MESH)

    @pl.loop(1, nz)
    def _(j):
        pl.semaphore_signal(barrier, inc=1, device_id=along_z(lax.rem(t + j, nz)), device_id_type=MESH)

    pl.semaphore_wait(barrier, nq + nz)

    below = [(d, j) for d in range(1, half) for j in (0, 1)] + [(half, 0)]
    above = [(d, 1 - j) for d, j in below]
    steps = len(below)

    def y_copy(n, way):
        d, j = (below if way > 0 else above)[n]
        src, dst = (-(d - 1) * way) % ny, (-d * way) % ny
        return remote(panels.at[src, j], panels.at[dst, j], y_ss.at[n, (1 - way) // 2], y_rs.at[n, (1 - way) // 2],
                      along_y(way))

    def y_step(n):
        for way in (1, -1):
            y_copy(n, way).wait_recv()
            if n + 2 < steps:
                y_copy(n + 2, way).start()

    loads[0].wait()
    loads[1].wait()
    for n in (0, 1):
        y_copy(n, 1).start()
        y_copy(n, -1).start()

    ids = ids_ref[...]
    one_hot = (lax.broadcasted_iota(jnp.int32, (2 * nq * ny, rows), 0) == ids).astype(F32)
    earlier = (lax.broadcasted_iota(jnp.int32, (rows, rows), 0)
               < lax.broadcasted_iota(jnp.int32, (rows, rows), 1)).astype(F32).astype(BF16)
    before = jnp.dot(one_hot.astype(BF16), earlier, preferred_element_type=F32)
    rank = jnp.sum(before * one_hot, axis=0, keepdims=True)
    second, core = lax.rem(ids, 2), lax.rem(lax.div(ids, 2), 2)
    home_y, home_x = lax.rem(lax.div(ids, 4), ny), lax.div(ids, 4 * ny)
    off = lax.rem(home_y - my + ny, ny)
    at = second * CAP
    for e, (b, i) in where_back.items():
        at = at + jnp.where(off == e, begin[b] + i * slots + (home_x * 2 + core) * (len(back[b]) * slots), 0)
    slot = at.astype(F32) + rank
    total = place.shape[0]
    place[...] = (lax.broadcasted_iota(jnp.int32, (total, rows), 0).astype(F32) == slot).astype(F32).astype(BF16)

    loads[2].wait()
    cols = min(256, width)
    for c in range(width // cols):
        send[:, c * cols:(c + 1) * cols] = jnp.dot(
            place[...], tok[:, c * cols:(c + 1) * cols], preferred_element_type=F32).astype(BF16)

    def block(b, q):
        span = len(back[b]) * slots
        return pl.ds(pl.multiple_of(begin[b] + q * span, span), span)

    def x_copy(b, q, at_q):
        return remote(send.at[block(b, q)], recv.at[block(b, at_q)], x_ss.at[b, q], x_rs.at[b, at_q], along_x(q))

    for b in range(len(back)):
        @pl.loop(1, nq)
        def _(j):
            x_copy(b, lax.rem(mq + j, nq), mq).start()

        recv[block(b, mq)] = send[block(b, mq)]

    def base_parts():
        loads[3].wait()
        for c in range(nz // 2):
            g = jnp.dot(tok[...], w[:, c * 2 * feat:(c + 1) * 2 * feat], preferred_element_type=F32)
            part[2 * c] = g[:, :feat]
            part[2 * c + 1] = g[:, feat:]

    def z_copy(s, way):
        k = (1 - way) // 2
        return remote(zs.at[k, s], zr.at[k, s], z_ss.at[k, s], z_rs.at[k, s], along_z(lax.rem(t + way + nz, nz)))

    def z_step(s):
        for way, hops in ((1, hz), (-1, hz - 1)):
            if s >= hops:
                continue
            k = (1 - way) // 2
            v = part[lax.rem(t + way * (hops - s) + nz, nz)]
            if s > 0:
                z_copy(s - 1, way).wait_recv()
                v = v + zr[k, s - 1].astype(F32)
            zs[k, s] = v.astype(BF16)
            z_copy(s, way).start()

    top = lax.broadcasted_iota(jnp.int32, (nx, slots, 2 * rk), 1) < CAP
    first = lax.broadcasted_iota(jnp.int32, (nx, slots, 2 * rk), 2) < rk

    def swap(v):
        return jnp.concatenate([v[:, CAP:], v[:, :CAP]], axis=1)

    def x_wait(b):
        @pl.loop(1, nq)
        def _(j):
            q = lax.rem(mq + j, nq)
            x_copy(b, q, q).wait_recv()

    def rank_part(offs):
        b, i = where_back[offs[0]]
        lo = i // 2 * 2 * slots
        span = len(back[b]) * slots
        x = recv[begin[b]:begin[b] + nq * span, :].reshape(nq, span, width)[:, lo:lo + 2 * slots]
        x = x.reshape(nq * 2 * slots, width)
        down = jnp.concatenate([panels[e, j, :, :width] for e in offs for j in (0, 1)], axis=0)
        r = lax.dot_general(x, down, (((1,), (1,)), ((), ())), preferred_element_type=F32)
        r = r.reshape(nq, 2 * slots, len(offs) * 2 * rk)
        for n, e in enumerate(offs):
            s = where_back[e][1] % 2
            v = r[:, s * slots:(s + 1) * slots, n * 2 * rk:(n + 1) * 2 * rk].reshape(nx, 2, slots, 2 * rk)
            even, odd = v[:, 0], v[:, 1]
            packed = jnp.where(top, jnp.where(first, even, swap(even)), jnp.where(first, swap(odd), odd))
            packed = packed.reshape(nx * slots, 2 * rk)
            rown[order.index(e)] = packed
            rsend[order.index(e)] = packed.astype(BF16)

    def these(b):
        return pl.ds(order.index(over_z[b][0]), len(over_z[b]))

    def rank_copy(b, p, at_p):
        return remote(rsend.at[these(b)], rrecv.at[at_p, these(b)], r_ss.at[b, p], r_rs.at[b, at_p], along_z(p))

    def rank_send(b):
        pairs = [over_z[b][:1], over_z[b][1:]] if len(over_z[b]) % 2 else [over_z[b]]
        for offs in pairs:
            if offs:
                rank_part(offs)

        @pl.loop(1, nz)
        def _(j):
            rank_copy(b, lax.rem(t + j, nz), t).start()

        rrecv[t, these(b)] = jnp.zeros((len(over_z[b]), nx * slots, 2 * rk), BF16)

    def lora_copy(b, q, at_q):
        return remote(lsend.at[block(b, q)], lrecv.at[block(b, at_q)], l_ss.at[b, q], l_rs.at[b, at_q], along_x(q))

    def widen(b):
        @pl.loop(1, nz)
        def _(j):
            p = lax.rem(t + j, nz)
            rank_copy(b, p, p).wait_recv()

        for e in over_z[b]:
            n = order.index(e)
            v = rown[n]
            for p in range(nz):
                v = v + rrecv[p, n].astype(F32)
            v = v.reshape(nx, slots, 2 * rk)
            zero = jnp.zeros_like(v)
            other = swap(v)
            even = jnp.where(top, jnp.where(first, v, zero), jnp.where(first, zero, other))
            odd = jnp.where(top, jnp.where(first, other, zero), jnp.where(first, zero, v))
            lhs = jnp.concatenate([even[:, None], odd[:, None]], axis=1).reshape(nq * slots, 2 * rk)
            high = lhs.astype(BF16)
            low = (lhs - high.astype(F32)).astype(BF16)
            ups = jnp.concatenate([panels[e, j, :, width:] for j in (0, 1)] * 2, axis=0)
            g = jnp.dot(jnp.concatenate([high, low], axis=1), ups, preferred_element_type=F32)
            widened[e] = g.reshape(nq, slots, feat)
        done = [e for o in over_z[:b + 1] for e in o]
        for k, offs in enumerate(back):
            if set(offs) <= set(done) and not set(offs) <= set(done) - set(over_z[b]):
                g = jnp.concatenate([widened[e] for e in offs], axis=1).astype(BF16)
                lsend[begin[k]:begin[k] + nq * len(offs) * slots, :] = g.reshape(nq * len(offs) * slots, feat)

                @pl.loop(1, nq)
                def _(j):
                    lora_copy(k, lax.rem(mq + j, nq), mq).start()

                lrecv[block(k, mq)] = lsend[block(k, mq)]

    def lora_add(b):
        @pl.loop(1, nq)
        def _(j):
            q = lax.rem(mq + j, nq)
            lora_copy(b, q, q).wait_recv()

        lo, n = begin[b], nq * len(back[b]) * slots
        return lax.dot_general(lrecv[lo:lo + n, :], place[lo:lo + n, :], (((0,), (0,)), ((), ())),
                               preferred_element_type=F32)

    last = len(over_z) - 1
    z_at = {0: 0, 2: 1, 4: 2, 5: 3}
    z_done = w_done = 0
    for n in range(steps):
        y_step(n)
        if n == 0:
            base_parts()
        if n in z_at and z_at[n] < hz:
            z_step(z_at[n])
            z_done = z_at[n] + 1
        if n == 1:
            for b in range(len(back)):
                x_wait(b)
        if n % 2 == 1:
            rank_send(n // 2)
        if n >= 4 and n < steps - 1:
            widen(w_done)
            w_done += 1
    rank_send(last)
    for s in range(z_done, hz):
        z_step(s)
    acc = part[t]
    for way, hops in ((1, hz), (-1, hz - 1)):
        z_copy(hops - 1, way).wait_recv()
        acc = acc + zr[(1 - way) // 2, hops - 1].astype(F32)
    acc = acc.T
    for b in range(w_done, last):
        widen(b)
    if len(back) > 2:
        acc = acc + lora_add(0)
    widen(last)
    acc = acc + lora_add(len(back) - 2)
    out_ref[...] = (acc + lora_add(len(back) - 1)).astype(BF16)

    for n in range(steps):
        y_copy(n, 1).wait_send()
        y_copy(n, -1).wait_send()
    for way, hops in ((1, hz), (-1, hz - 1)):
        for s in range(hops):
            z_copy(s, way).wait_send()
    for b in range(len(back)):
        @pl.loop(1, nq)
        def _(j):
            q = lax.rem(mq + j, nq)
            x_copy(b, q, mq).wait_send()
            lora_copy(b, q, mq).wait_send()
    for b in range(len(over_z)):
        @pl.loop(1, nz)
        def _(j):
            rank_copy(b, lax.rem(t + j, nz), t).wait_send()


def local(dims, tokens, w_key, row_adapter, panel_a, up_panels):
    nx, ny, nz = dims
    rows, width = tokens.shape
    feat = w_key.shape[1] // nz
    rk = panel_a.shape[2]
    nq, hz = 2 * nx, nz // 2
    over_z, back = batches(ny)
    total = ny * nq * 2 * CAP
    vmem = pl.BlockSpec(memory_space=pltpu.VMEM)
    hbm = pl.BlockSpec(memory_space=pl.ANY)
    dma = pltpu.SemaphoreType.DMA
    tiles = (ny, nx * 2 * CAP, 2 * rk)
    return pl.pallas_call(
        functools.partial(kernel, dims),
        out_shape=jax.ShapeDtypeStruct((feat, rows), BF16),
        in_specs=[vmem, hbm, hbm, hbm, hbm],
        out_specs=vmem,
        scratch_shapes=[
            pltpu.VMEM((rows, width), BF16),
            pltpu.VMEM(w_key.shape, BF16),
            pltpu.VMEM((ny, 2, rk, width + feat), BF16),
            pltpu.VMEM((total, rows), BF16),
            pltpu.VMEM((total, width), BF16),
            pltpu.VMEM((total, width), BF16),
            pltpu.VMEM((nz, rows, feat), F32),
            pltpu.VMEM((2, hz, rows, feat), BF16),
            pltpu.VMEM((2, hz, rows, feat), BF16),
            pltpu.VMEM(tiles, BF16),
            pltpu.VMEM((nz, *tiles), BF16),
            pltpu.VMEM(tiles, F32),
            pltpu.VMEM((ny, nq, 2 * CAP, feat), F32),
            pltpu.VMEM((total, feat), BF16),
            pltpu.VMEM((total, feat), BF16),
            dma((4,)),
            dma((ny - 1, 2)),
            dma((ny - 1, 2)),
            dma((len(back), nq)),
            dma((len(back), nq)),
            dma((2, hz)),
            dma((2, hz)),
            dma((len(over_z), nz)),
            dma((len(over_z), nz)),
            dma((len(back), nq)),
            dma((len(back), nq)),
        ],
        compiler_params=pltpu.CompilerParams(
            collective_id=0, has_side_effects=True, vmem_limit_bytes=62 * 1024 * 1024),
    )(row_adapter.reshape(1, rows), tokens, w_key, jnp.swapaxes(panel_a, 1, 2), up_panels)


def solution(mesh):
    return jax.shard_map(
        functools.partial(local, (X, Y, mesh.shape["tensor"])),
        mesh=mesh,
        in_specs=(
            P("group", "tensor"),
            P("tensor", None),
            P("group", None),
            P("group", "tensor", None),
            P("group", None, None),
        ),
        out_specs=P("tensor", "group"),
        check_vma=False,
    )
```

```python
import functools

import jax
import jax.numpy as jnp
from jax import lax
from jax.experimental import pallas as pl
from jax.experimental.pallas import tpu as pltpu
from jax.sharding import PartitionSpec as P

MESH = pl.DeviceIdType.MESH
F32, BF16 = jnp.float32, jnp.bfloat16
X, Y = 4, 8
CAP = 4

def batches(ny):
    half = ny // 2
    over_z = [[d, ny - d] for d in range(1, half - 1)] + [[0, half - 1, half + 1], [half]]
    early = [e for d in range(1, half - 1) for e in (d, ny - d)]
    back = ([early] if early else []) + [[half - 1, half + 1], [0, half]]
    return over_z, back


def kernel(dims, ids_hbm, tok_hbm, w_hbm, pa_hbm, up_hbm, out_ref,
           ids_ref, tok, w, panels, place, send, recv, part, zs, zr, rsend, rrecv, rown, widened, lsend, lrecv,
           in_sem, y_ss, y_rs, x_ss, x_rs, z_ss, z_rs, r_ss, r_rs, l_ss, l_rs):
    nx, ny, nz = dims
    nq = 2 * nx
    half = ny // 2
    rows, width = tok.shape
    feat = out_ref.shape[0]
    rk = panels.shape[2]
    slots = 2 * CAP
    over_z, back = batches(ny)
    order = [e for b in over_z for e in b]
    begin, where_back = [], {}
    for b, offs in enumerate(back):
        begin.append(sum(len(o) for o in back[:b]) * nq * slots)
        for i, e in enumerate(offs):
            where_back[e] = (b, i)

    me, t = lax.axis_index("group"), lax.axis_index("tensor")
    mc, my, mx = lax.rem(me, 2), lax.rem(lax.div(me, 2), ny), lax.div(me, 2 * ny)
    mq = mx * 2 + mc

    def along_x(q):
        return {"group": (lax.div(q, 2) * ny + my) * 2 + lax.rem(q, 2)}

    def along_y(step):
        return {"group": (mx * ny + lax.rem(my + step + ny, ny)) * 2 + mc}

    def along_z(p):
        return {"tensor": p}

    def remote(src, dst, ss, rs, where):
        return pltpu.make_async_remote_copy(src, dst, ss, rs, device_id=where, device_id_type=MESH)

    barrier = pltpu.get_barrier_semaphore()
    for step in (-1, 1):
        pl.semaphore_signal(barrier, inc=1, device_id=along_y(step), device_id_type=MESH)

    mine = pl.ds(pl.multiple_of(t * feat, feat), feat)
    loads = [
        pltpu.make_async_copy(pa_hbm, panels.at[0, :, :, pl.ds(0, width)], in_sem.at[0]),
        pltpu.make_async_copy(up_hbm.at[:, :, mine], panels.at[0, :, :, pl.ds(width, feat)], in_sem.at[1]),
        pltpu.make_async_copy(tok_hbm, tok, in_sem.at[2]),
        pltpu.make_async_copy(ids_hbm, ids_ref, in_sem.at[4]),
        pltpu.make_async_copy(w_hbm, w, in_sem.at[3]),
    ]
    for c in loads:
        c.start()

    @pl.loop(1, nq)
    def _(j):
        pl.semaphore_signal(barrier, inc=1, device_id=along_x(lax.rem(mq + j, nq)), device_id_type=MESH)

    @pl.loop(1, nz)
    def _(j):
        pl.semaphore_signal(barrier, inc=1, device_id=along_z(lax.rem(t + j, nz)), device_id_type=MESH)

    pl.semaphore_wait(barrier, nq + nz)

    below = [(d, j) for d in range(1, half) for j in (0, 1)] + [(half, 0)]
    above = [(d, 1 - j) for d, j in below]
    steps = len(below)

    def y_copy(n, way):
        d, j = (below if way > 0 else above)[n]
        src, dst = (-(d - 1) * way) % ny, (-d * way) % ny
        return remote(panels.at[src, j], panels.at[dst, j], y_ss.at[n, (1 - way) // 2], y_rs.at[n, (1 - way) // 2],
                      along_y(way))

    def y_step(n):
        for way in (1, -1):
            y_copy(n, way).wait_recv()
            if n + 2 < steps:
                y_copy(n + 2, way).start()

    loads[0].wait()
    loads[1].wait()
    for n in (0, 1):
        y_copy(n, 1).start()
        y_copy(n, -1).start()

    loads[3].wait()
    ids = ids_ref[...]
    one_hot = (lax.broadcasted_iota(jnp.int32, (2 * nq * ny, rows), 0) == ids).astype(F32)
    earlier = (lax.broadcasted_iota(jnp.int32, (rows, rows), 0)
               < lax.broadcasted_iota(jnp.int32, (rows, rows), 1)).astype(F32).astype(BF16)
    before = jnp.dot(one_hot.astype(BF16), earlier, preferred_element_type=F32)
    rank = jnp.sum(before * one_hot, axis=0, keepdims=True)
    second, core = lax.rem(ids, 2), lax.rem(lax.div(ids, 2), 2)
    home_y, home_x = lax.rem(lax.div(ids, 4), ny), lax.div(ids, 4 * ny)
    off = lax.rem(home_y - my + ny, ny)
    at = second * CAP
    for e, (b, i) in where_back.items():
        at = at + jnp.where(off == e, begin[b] + i * slots + (home_x * 2 + core) * (len(back[b]) * slots), 0)
    slot = at.astype(F32) + rank
    total = place.shape[0]
    place[...] = (lax.broadcasted_iota(jnp.int32, (total, rows), 0).astype(F32) == slot).astype(F32).astype(BF16)

    loads[2].wait()
    cols = min(256, width)
    for c in range(width // cols):
        send[:, c * cols:(c + 1) * cols] = jnp.dot(
            place[...], tok[:, c * cols:(c + 1) * cols], preferred_element_type=F32).astype(BF16)

    def block(b, q):
        span = len(back[b]) * slots
        return pl.ds(pl.multiple_of(begin[b] + q * span, span), span)

    def x_copy(b, q, at_q):
        return remote(send.at[block(b, q)], recv.at[block(b, at_q)], x_ss.at[b, q], x_rs.at[b, at_q], along_x(q))

    for b in range(len(back)):
        @pl.loop(1, nq)
        def _(j):
            x_copy(b, lax.rem(mq + j, nq), mq).start()

        recv[block(b, mq)] = send[block(b, mq)]

    def base_parts():
        loads[4].wait()
        for c in range(nz // 2):
            g = jnp.dot(tok[...], w[:, c * 2 * feat:(c + 1) * 2 * feat], preferred_element_type=F32)
            part[2 * c] = g[:, :feat]
            part[2 * c + 1] = g[:, feat:]

    turn = 1 - 2 * lax.rem(t, 2)

    def at_z(step):
        return lax.rem(t + step * turn + nz, nz)

    def z_copy(n):
        to = (2, -1, 1, -1, 1, 2, -2)[n]
        return remote(zs.at[n], zr.at[n], z_ss.at[n], z_rs.at[n], along_z(at_z(to)))

    def z_send(n, v):
        zs[n] = v.astype(BF16)
        z_copy(n).start()

    def z_first():
        for n, target in enumerate((4, -3, 3, -1, 1)):
            z_send(n, part[at_z(target)])

    def z_second():
        z_copy(0).wait_recv()
        z_copy(1).wait_recv()
        z_send(5, part[at_z(2)] + zr[0].astype(F32) + zr[1].astype(F32))
        z_copy(2).wait_recv()
        z_send(6, part[at_z(-2)] + zr[2].astype(F32))

    top = lax.broadcasted_iota(jnp.int32, (nx, slots, 2 * rk), 1) < CAP
    first = lax.broadcasted_iota(jnp.int32, (nx, slots, 2 * rk), 2) < rk

    def swap(v):
        return jnp.concatenate([v[:, CAP:], v[:, :CAP]], axis=1)

    def x_wait(b):
        @pl.loop(1, nq)
        def _(j):
            q = lax.rem(mq + j, nq)
            x_copy(b, q, q).wait_recv()

    def rank_part(offs):
        b, i = where_back[offs[0]]
        lo = i // 2 * 2 * slots
        span = len(back[b]) * slots
        x = recv[begin[b]:begin[b] + nq * span, :].reshape(nq, span, width)[:, lo:lo + 2 * slots]
        x = x.reshape(nq * 2 * slots, width)
        down = jnp.concatenate([panels[e, j, :, :width] for e in offs for j in (0, 1)], axis=0)
        r = lax.dot_general(x, down, (((1,), (1,)), ((), ())), preferred_element_type=F32)
        r = r.reshape(nq, 2 * slots, len(offs) * 2 * rk)
        for n, e in enumerate(offs):
            s = where_back[e][1] % 2
            v = r[:, s * slots:(s + 1) * slots, n * 2 * rk:(n + 1) * 2 * rk].reshape(nx, 2, slots, 2 * rk)
            even, odd = v[:, 0], v[:, 1]
            packed = jnp.where(top, jnp.where(first, even, swap(even)), jnp.where(first, swap(odd), odd))
            packed = packed.reshape(nx * slots, 2 * rk)
            rown[order.index(e)] = packed
            rsend[order.index(e)] = packed.astype(BF16)

    def these(b):
        return pl.ds(order.index(over_z[b][0]), len(over_z[b]))

    def rank_copy(b, p, at_p):
        return remote(rsend.at[these(b)], rrecv.at[at_p, these(b)], r_ss.at[b, p], r_rs.at[b, at_p], along_z(p))

    def rank_send(b):
        pairs = [over_z[b][:1], over_z[b][1:]] if len(over_z[b]) % 2 else [over_z[b]]
        for offs in pairs:
            if offs:
                rank_part(offs)

        @pl.loop(1, nz)
        def _(j):
            rank_copy(b, lax.rem(t + j, nz), t).start()

        rrecv[t, these(b)] = jnp.zeros((len(over_z[b]), nx * slots, 2 * rk), BF16)

    def lora_copy(b, q, at_q):
        return remote(lsend.at[block(b, q)], lrecv.at[block(b, at_q)], l_ss.at[b, q], l_rs.at[b, at_q], along_x(q))

    def widen(b):
        @pl.loop(1, nz)
        def _(j):
            p = lax.rem(t + j, nz)
            rank_copy(b, p, p).wait_recv()

        for e in over_z[b]:
            n = order.index(e)
            v = rown[n]
            for p in range(nz):
                v = v + rrecv[p, n].astype(F32)
            v = v.reshape(nx, slots, 2 * rk)
            zero = jnp.zeros_like(v)
            other = swap(v)
            even = jnp.where(top, jnp.where(first, v, zero), jnp.where(first, zero, other))
            odd = jnp.where(top, jnp.where(first, other, zero), jnp.where(first, zero, v))
            lhs = jnp.concatenate([even[:, None], odd[:, None]], axis=1).reshape(nq * slots, 2 * rk)
            high = lhs.astype(BF16)
            low = (lhs - high.astype(F32)).astype(BF16)
            ups = jnp.concatenate([panels[e, j, :, width:] for j in (0, 1)] * 2, axis=0)
            g = jnp.dot(jnp.concatenate([high, low], axis=1), ups, preferred_element_type=F32)
            widened[e] = g.reshape(nq, slots, feat)
        done = [e for o in over_z[:b + 1] for e in o]
        for k, offs in enumerate(back):
            if set(offs) <= set(done) and not set(offs) <= set(done) - set(over_z[b]):
                g = jnp.concatenate([widened[e] for e in offs], axis=1).astype(BF16)
                lsend[begin[k]:begin[k] + nq * len(offs) * slots, :] = g.reshape(nq * len(offs) * slots, feat)

                @pl.loop(1, nq)
                def _(j):
                    lora_copy(k, lax.rem(mq + j, nq), mq).start()

                lrecv[block(k, mq)] = lsend[block(k, mq)]

    def lora_add(b):
        @pl.loop(1, nq)
        def _(j):
            q = lax.rem(mq + j, nq)
            lora_copy(b, q, q).wait_recv()

        lo, n = begin[b], nq * len(back[b]) * slots
        return lax.dot_general(lrecv[lo:lo + n, :], place[lo:lo + n, :], (((0,), (0,)), ((), ())),
                               preferred_element_type=F32)

    last = len(over_z) - 1
    waited = -1
    for n in range(steps):
        y_step(n)
        if n == 0:
            base_parts()
            z_first()
        if n == steps // 2:
            z_second()
        b = {2: 0, 3: 1, 5: 2, 6: 3}.get(n) if steps == 7 else {1: 0, 2: 1}.get(n)
        if b is not None:
            need = max(where_back[e][0] for e in over_z[b])
            while waited < need:
                waited += 1
                x_wait(waited)
            rank_send(b)
    acc = part[t]
    for n in (3, 4, 5, 6):
        z_copy(n).wait_recv()
        acc = acc + zr[n].astype(F32)
    acc = acc.T
    for b in range(last + 1):
        widen(b)
    for b in range(len(back)):
        acc = acc + lora_add(b)
    out_ref[...] = acc.astype(BF16)

    for n in range(steps):
        y_copy(n, 1).wait_send()
        y_copy(n, -1).wait_send()
    for n in range(7):
        z_copy(n).wait_send()
    for b in range(len(back)):
        @pl.loop(1, nq)
        def _(j):
            q = lax.rem(mq + j, nq)
            x_copy(b, q, mq).wait_send()
            lora_copy(b, q, mq).wait_send()
    for b in range(len(over_z)):
        @pl.loop(1, nz)
        def _(j):
            rank_copy(b, lax.rem(t + j, nz), t).wait_send()


def local(dims, tokens, w_key, row_adapter, panel_a, up_panels):
    nx, ny, nz = dims
    rows, width = tokens.shape
    feat = w_key.shape[1] // nz
    rk = panel_a.shape[2]
    nq = 2 * nx
    over_z, back = batches(ny)
    total = ny * nq * 2 * CAP
    vmem = pl.BlockSpec(memory_space=pltpu.VMEM)
    hbm = pl.BlockSpec(memory_space=pl.ANY)
    dma = pltpu.SemaphoreType.DMA
    tiles = (ny, nx * 2 * CAP, 2 * rk)
    return pl.pallas_call(
        functools.partial(kernel, dims),
        out_shape=jax.ShapeDtypeStruct((feat, rows), BF16),
        in_specs=[hbm] * 5,
        out_specs=vmem,
        scratch_shapes=[
            pltpu.VMEM((1, rows), jnp.int32),
            pltpu.VMEM((rows, width), BF16),
            pltpu.VMEM(w_key.shape, BF16),
            pltpu.VMEM((ny, 2, rk, width + feat), BF16),
            pltpu.VMEM((total, rows), BF16),
            pltpu.VMEM((total, width), BF16),
            pltpu.VMEM((total, width), BF16),
            pltpu.VMEM((nz, rows, feat), F32),
            pltpu.VMEM((7, rows, feat), BF16),
            pltpu.VMEM((7, rows, feat), BF16),
            pltpu.VMEM(tiles, BF16),
            pltpu.VMEM((nz, *tiles), BF16),
            pltpu.VMEM(tiles, F32),
            pltpu.VMEM((ny, nq, 2 * CAP, feat), F32),
            pltpu.VMEM((total, feat), BF16),
            pltpu.VMEM((total, feat), BF16),
            dma((5,)),
            dma((ny - 1, 2)),
            dma((ny - 1, 2)),
            dma((len(back), nq)),
            dma((len(back), nq)),
            dma((7,)),
            dma((7,)),
            dma((len(over_z), nz)),
            dma((len(over_z), nz)),
            dma((len(back), nq)),
            dma((len(back), nq)),
        ],
        compiler_params=pltpu.CompilerParams(
            collective_id=0, has_side_effects=True, vmem_limit_bytes=62 * 1024 * 1024),
    )(row_adapter.reshape(1, rows), tokens, w_key, jnp.swapaxes(panel_a, 1, 2), up_panels)


def solution(mesh):
    return jax.shard_map(
        functools.partial(local, (X, Y, mesh.shape["tensor"])),
        mesh=mesh,
        in_specs=(
            P("group", "tensor"),
            P("tensor", None),
            P("group", None),
            P("group", "tensor", None),
            P("group", None, None),
        ),
        out_specs=P("tensor", "group"),
        check_vma=False,
    )
```

```python
import functools

import jax
import jax.numpy as jnp
from jax import lax
from jax.experimental import pallas as pl
from jax.experimental.pallas import tpu as pltpu
from jax.sharding import PartitionSpec as P

MESH = pl.DeviceIdType.MESH
F32, BF16 = jnp.float32, jnp.bfloat16
X, Y = 4, 8
CAP = 4

def batches(ny):
    half = ny // 2
    over_z = [[e for d in range(1, half - 1) for e in (d, ny - d)], [0], [half - 1, half + 1], [half]]
    early = [e for d in range(1, half - 1) for e in (d, ny - d)]
    back = ([early] if early else []) + [[half - 1, half + 1], [0, half]]
    return over_z, back


def kernel(dims, ids_hbm, tok_hbm, w_hbm, pa_hbm, up_hbm, out_ref,
           ids_ref, tok, w, panels, ups, place, send, recv, part, zs, zr, rsend, rrecv, rown, srecv, full, widened, lsend, lrecv,
           in_sem, y_ss, y_rs, u_ss, u_rs, x_ss, x_rs, z_ss, z_rs, r_ss, r_rs, s_ss, s_rs, a_ss, a_rs, l_ss, l_rs):
    nx, ny, nz = dims
    nq = 2 * nx
    half = ny // 2
    rows, width = tok.shape
    feat = out_ref.shape[0]
    rk = panels.shape[2]
    slots = 2 * CAP
    over_z, back = batches(ny)
    order = [e for b in over_z for e in b]
    begin, where_back = [], {}
    for b, offs in enumerate(back):
        begin.append(sum(len(o) for o in back[:b]) * nq * slots)
        for i, e in enumerate(offs):
            where_back[e] = (b, i)

    me, t = lax.axis_index("group"), lax.axis_index("tensor")
    mc, my, mx = lax.rem(me, 2), lax.rem(lax.div(me, 2), ny), lax.div(me, 2 * ny)
    mq = mx * 2 + mc

    def along_x(q):
        return {"group": (lax.div(q, 2) * ny + my) * 2 + lax.rem(q, 2)}

    def along_y(step):
        return {"group": (mx * ny + lax.rem(my + step + ny, ny)) * 2 + mc}

    def along_z(p):
        return {"tensor": p}

    def remote(src, dst, ss, rs, where):
        return pltpu.make_async_remote_copy(src, dst, ss, rs, device_id=where, device_id_type=MESH)

    barrier = pltpu.get_barrier_semaphore()
    for step in (-1, 1, ny // 2):
        pl.semaphore_signal(barrier, inc=1, device_id=along_y(step), device_id_type=MESH)

    mine = pl.ds(pl.multiple_of(t * feat, feat), feat)
    loads = [
        pltpu.make_async_copy(pa_hbm, panels.at[0], in_sem.at[0]),
        pltpu.make_async_copy(up_hbm.at[:, :, mine], ups.at[0], in_sem.at[1]),
        pltpu.make_async_copy(tok_hbm, tok, in_sem.at[2]),
        pltpu.make_async_copy(ids_hbm, ids_ref, in_sem.at[4]),
        pltpu.make_async_copy(w_hbm, w, in_sem.at[3]),
    ]
    for c in loads:
        c.start()

    @pl.loop(1, nq)
    def _(j):
        pl.semaphore_signal(barrier, inc=1, device_id=along_x(lax.rem(mq + j, nq)), device_id_type=MESH)

    @pl.loop(1, nz)
    def _(j):
        pl.semaphore_signal(barrier, inc=1, device_id=along_z(lax.rem(t + j, nz)), device_id_type=MESH)

    pl.semaphore_wait(barrier, nq + nz + 1)

    below = [(d, j) for d in range(1, half) for j in (0, 1)] + [(half, 0)]
    above = [(d, 1 - j) for d, j in below]
    steps = len(below)

    def y_copy(n, way):
        d, j = (below if way > 0 else above)[n]
        src, dst = (-(d - 1) * way) % ny, (-d * way) % ny
        return remote(panels.at[src, j], panels.at[dst, j], y_ss.at[n, (1 - way) // 2], y_rs.at[n, (1 - way) // 2],
                      along_y(way))

    def y_step(n):
        for way in (1, -1):
            y_copy(n, way).wait_recv()
            if n + 2 < steps:
                y_copy(n + 2, way).start()

    def u_copy(d, way):
        src, dst = (-(d - 1) * way) % ny, (-d * way) % ny
        return remote(ups.at[src], ups.at[dst], u_ss.at[d, (1 - way) // 2], u_rs.at[d, (1 - way) // 2], along_y(way))

    def u_across():
        return remote(ups.at[0], ups.at[half], u_ss.at[half, 0], u_rs.at[half, 0], along_y(half))

    def u_step(d):
        for way in (1, -1):
            if d > 0:
                u_copy(d, way).wait_recv()
            if d < half - 1:
                u_copy(d + 1, way).start()

    loads[0].wait()
    for n in (0, 1):
        y_copy(n, 1).start()
        y_copy(n, -1).start()
    loads[1].wait()

    loads[3].wait()
    ids = ids_ref[...]
    one_hot = (lax.broadcasted_iota(jnp.int32, (2 * nq * ny, rows), 0) == ids).astype(F32)
    earlier = (lax.broadcasted_iota(jnp.int32, (rows, rows), 0)
               < lax.broadcasted_iota(jnp.int32, (rows, rows), 1)).astype(F32).astype(BF16)
    before = jnp.dot(one_hot.astype(BF16), earlier, preferred_element_type=F32)
    rank = jnp.sum(before * one_hot, axis=0, keepdims=True)
    second, core = lax.rem(ids, 2), lax.rem(lax.div(ids, 2), 2)
    home_y, home_x = lax.rem(lax.div(ids, 4), ny), lax.div(ids, 4 * ny)
    off = lax.rem(home_y - my + ny, ny)
    at = second * CAP
    for e, (b, i) in where_back.items():
        at = at + jnp.where(off == e, begin[b] + i * slots + (home_x * 2 + core) * (len(back[b]) * slots), 0)
    slot = at.astype(F32) + rank
    total = place.shape[0]
    place[...] = (lax.broadcasted_iota(jnp.int32, (total, rows), 0).astype(F32) == slot).astype(F32).astype(BF16)

    loads[2].wait()
    cols = min(256, width)
    for c in range(width // cols):
        send[:, c * cols:(c + 1) * cols] = jnp.dot(
            place[...], tok[:, c * cols:(c + 1) * cols], preferred_element_type=F32).astype(BF16)

    def block(b, q):
        span = len(back[b]) * slots
        return pl.ds(pl.multiple_of(begin[b] + q * span, span), span)

    def x_copy(b, q, at_q):
        return remote(send.at[block(b, q)], recv.at[block(b, at_q)], x_ss.at[b, q], x_rs.at[b, at_q], along_x(q))

    for b in (0, 2, 1):
        @pl.loop(1, nq)
        def _(j):
            x_copy(b, lax.rem(mq + j, nq), mq).start()

        recv[block(b, mq)] = send[block(b, mq)]

    def base_parts():
        loads[4].wait()
        for c in range(nz // 2):
            g = jnp.dot(tok[...], w[:, c * 2 * feat:(c + 1) * 2 * feat], preferred_element_type=F32)
            part[2 * c] = g[:, :feat]
            part[2 * c + 1] = g[:, feat:]

    turn = 1 - 2 * lax.rem(t, 2)

    def at_z(step):
        return lax.rem(t + step * turn + nz, nz)

    def z_copy(n):
        to = (2, -1, 1, -1, 1, 2, -2)[n]
        return remote(zs.at[n], zr.at[n], z_ss.at[n], z_rs.at[n], along_z(at_z(to)))

    def z_send(n, v):
        zs[n] = v.astype(BF16)
        z_copy(n).start()

    def z_first():
        for n, target in enumerate((4, -3, 3, -1, 1)):
            z_send(n, part[at_z(target)])

    def z_second():
        z_copy(0).wait_recv()
        z_copy(1).wait_recv()
        z_send(5, part[at_z(2)] + zr[0].astype(F32) + zr[1].astype(F32))
        z_copy(2).wait_recv()
        z_send(6, part[at_z(-2)] + zr[2].astype(F32))

    top = lax.broadcasted_iota(jnp.int32, (nx, slots, 2 * rk), 1) < CAP
    first = lax.broadcasted_iota(jnp.int32, (nx, slots, 2 * rk), 2) < rk

    def swap(v):
        return jnp.concatenate([v[:, CAP:], v[:, :CAP]], axis=1)

    def x_wait(b):
        @pl.loop(1, nq)
        def _(j):
            q = lax.rem(mq + j, nq)
            x_copy(b, q, q).wait_recv()

    def rank_part(offs):
        b, i = where_back[offs[0]]
        lo = i // 2 * 2 * slots
        span = len(back[b]) * slots
        x = recv[begin[b]:begin[b] + nq * span, :].reshape(nq, span, width)[:, lo:lo + 2 * slots]
        x = x.reshape(nq * 2 * slots, width)
        down = jnp.concatenate([panels[e, j] for e in offs for j in (0, 1)], axis=0)
        r = lax.dot_general(x, down, (((1,), (1,)), ((), ())), preferred_element_type=F32)
        r = r.reshape(nq, 2 * slots, len(offs) * 2 * rk)
        for n, e in enumerate(offs):
            s = where_back[e][1] % 2
            v = r[:, s * slots:(s + 1) * slots, n * 2 * rk:(n + 1) * 2 * rk].reshape(nx, 2, slots, 2 * rk)
            even, odd = v[:, 0], v[:, 1]
            packed = jnp.where(top, jnp.where(first, even, swap(even)), jnp.where(first, swap(odd), odd))
            packed = packed.reshape(nx * slots, 2 * rk)
            rown[order.index(e)] = packed
            rsend[order.index(e)] = packed.astype(BF16)

    def these(b):
        return pl.ds(order.index(over_z[b][0]), len(over_z[b]))

    def rank_copy(b, p, at_p):
        return remote(rsend.at[these(b)], rrecv.at[at_p, these(b)], r_ss.at[b, p], r_rs.at[b, at_p], along_z(p))

    def rank_send(b):
        @pl.loop(1, nz)
        def _(j):
            rank_copy(b, lax.rem(t + j, nz), t).start()

        rrecv[t, these(b)] = jnp.zeros((len(over_z[b]), nx * slots, 2 * rk), BF16)

    share = len(over_z[0]) * nx * slots // nz
    shares = nx * slots // share

    def rows_of(p):
        return lax.div(p, shares), pl.ds(pl.multiple_of(lax.rem(p, shares) * share, share), share)

    def sum_copy(p, at_p):
        return remote(rsend.at[rows_of(p)], srecv.at[at_p], s_ss.at[p], s_rs.at[at_p], along_z(p))

    def full_copy(p, at_p):
        return remote(full.at[at_p], full.at[at_p], a_ss.at[p], a_rs.at[at_p], along_z(p))

    def sum_send():
        @pl.loop(1, nz)
        def _(j):
            sum_copy(lax.rem(t + j, nz), t).start()

        srecv[t] = jnp.zeros((share, 2 * rk), BF16)

    def full_send():
        @pl.loop(1, nz)
        def _(j):
            p = lax.rem(t + j, nz)
            sum_copy(p, p).wait_recv()

        v = rown[rows_of(t)]
        for p in range(nz):
            v = v + srecv[p].astype(F32)
        full[t] = v

        @pl.loop(1, nz)
        def _(j):
            full_copy(lax.rem(t + j, nz), t).start()

    def lora_copy(b, q, at_q):
        return remote(lsend.at[block(b, q)], lrecv.at[block(b, at_q)], l_ss.at[b, q], l_rs.at[b, at_q], along_x(q))

    def widen(b):
        @pl.loop(1, nz)
        def _(j):
            p = lax.rem(t + j, nz)
            (rank_copy(b, p, p) if b else full_copy(p, p)).wait_recv()

        for e in over_z[b]:
            n = order.index(e)
            if b == 0:
                v = full[n * shares:(n + 1) * shares]
            else:
                v = rown[n]
                for p in range(nz):
                    v = v + rrecv[p, n].astype(F32)
            v = v.reshape(nx, slots, 2 * rk)
            zero = jnp.zeros_like(v)
            other = swap(v)
            even = jnp.where(top, jnp.where(first, v, zero), jnp.where(first, zero, other))
            odd = jnp.where(top, jnp.where(first, other, zero), jnp.where(first, zero, v))
            lhs = jnp.concatenate([even[:, None], odd[:, None]], axis=1).reshape(nq * slots, 2 * rk)
            high = lhs.astype(BF16)
            low = (lhs - high.astype(F32)).astype(BF16)
            both = jnp.concatenate([ups[e, j] for j in (0, 1)] * 2, axis=0)
            g = jnp.dot(jnp.concatenate([high, low], axis=1), both, preferred_element_type=F32)
            widened[e] = g.reshape(nq, slots, feat)
        done = [e for o in over_z[:b + 1] for e in o]
        for k, offs in enumerate(back):
            if set(offs) <= set(done) and not set(offs) <= set(done) - set(over_z[b]):
                g = jnp.concatenate([widened[e] for e in offs], axis=1).astype(BF16)
                lsend[begin[k]:begin[k] + nq * len(offs) * slots, :] = g.reshape(nq * len(offs) * slots, feat)

                @pl.loop(1, nq)
                def _(j):
                    lora_copy(k, lax.rem(mq + j, nq), mq).start()

                lrecv[block(k, mq)] = lsend[block(k, mq)]

    def lora_add(b):
        @pl.loop(1, nq)
        def _(j):
            q = lax.rem(mq + j, nq)
            lora_copy(b, q, q).wait_recv()

        lo, n = begin[b], nq * len(back[b]) * slots
        return lax.dot_general(lrecv[lo:lo + n, :], place[lo:lo + n, :], (((0,), (0,)), ((), ())),
                               preferred_element_type=F32)

    last = len(over_z) - 1
    u_at = {2: 0, 4: 1, 6: 2}
    for n in range(steps):
        y_step(n)
        if n in u_at:
            u_step(u_at[n])
        if n == 5:
            u_across().start()
        if n == 0:
            base_parts()
            z_first()
        if n == steps // 2:
            z_second()
        if n == 2:
            x_wait(0)
            rank_part(over_z[0][:2])
        if n == 3:
            rank_part(over_z[0][2:])
            sum_send()
        if n == 4:
            x_wait(2)
            rank_part(over_z[1])
            rank_send(1)
        if n == 5:
            x_wait(1)
            rank_part(over_z[2])
            rank_send(2)
            full_send()
        if n == 6:
            rank_part(over_z[3])
            rank_send(3)
    acc = part[t]
    for n in (3, 4, 5, 6):
        z_copy(n).wait_recv()
        acc = acc + zr[n].astype(F32)
    acc = acc.T
    for b in range(last):
        if b == last - 1:
            for d in range(max(u_at.values()) + 1, half):
                u_step(d)
        widen(b)
    u_across().wait_recv()
    widen(last)
    for b in range(len(back)):
        acc = acc + lora_add(b)
    out_ref[...] = acc.astype(BF16)

    for n in range(steps):
        y_copy(n, 1).wait_send()
        y_copy(n, -1).wait_send()
    for d in range(1, half):
        u_copy(d, 1).wait_send()
        u_copy(d, -1).wait_send()
    u_across().wait_send()
    for n in range(7):
        z_copy(n).wait_send()
    for b in range(len(back)):
        @pl.loop(1, nq)
        def _(j):
            q = lax.rem(mq + j, nq)
            x_copy(b, q, mq).wait_send()
            lora_copy(b, q, mq).wait_send()
    for b in range(1, len(over_z)):
        @pl.loop(1, nz)
        def _(j):
            rank_copy(b, lax.rem(t + j, nz), t).wait_send()

    @pl.loop(1, nz)
    def _(j):
        p = lax.rem(t + j, nz)
        sum_copy(p, t).wait_send()
        full_copy(p, t).wait_send()


def local(dims, tokens, w_key, row_adapter, panel_a, up_panels):
    nx, ny, nz = dims
    rows, width = tokens.shape
    feat = w_key.shape[1] // nz
    rk = panel_a.shape[2]
    nq = 2 * nx
    over_z, back = batches(ny)
    total = ny * nq * 2 * CAP
    vmem = pl.BlockSpec(memory_space=pltpu.VMEM)
    hbm = pl.BlockSpec(memory_space=pl.ANY)
    dma = pltpu.SemaphoreType.DMA
    tiles = (ny, nx * 2 * CAP, 2 * rk)
    share = len(over_z[0]) * nx * 2 * CAP // nz
    return pl.pallas_call(
        functools.partial(kernel, dims),
        out_shape=jax.ShapeDtypeStruct((feat, rows), BF16),
        in_specs=[hbm] * 5,
        out_specs=vmem,
        scratch_shapes=[
            pltpu.VMEM((1, rows), jnp.int32),
            pltpu.VMEM((rows, width), BF16),
            pltpu.VMEM(w_key.shape, BF16),
            pltpu.VMEM((ny, 2, rk, width), BF16),
            pltpu.VMEM((ny, 2, rk, feat), BF16),
            pltpu.VMEM((total, rows), BF16),
            pltpu.VMEM((total, width), BF16),
            pltpu.VMEM((total, width), BF16),
            pltpu.VMEM((nz, rows, feat), F32),
            pltpu.VMEM((7, rows, feat), BF16),
            pltpu.VMEM((7, rows, feat), BF16),
            pltpu.VMEM(tiles, BF16),
            pltpu.VMEM((nz, *tiles), BF16),
            pltpu.VMEM(tiles, F32),
            pltpu.VMEM((nz, share, 2 * rk), BF16),
            pltpu.VMEM((nz, share, 2 * rk), F32),
            pltpu.VMEM((ny, nq, 2 * CAP, feat), F32),
            pltpu.VMEM((total, feat), BF16),
            pltpu.VMEM((total, feat), BF16),
            dma((5,)),
            dma((ny - 1, 2)),
            dma((ny - 1, 2)),
            dma((ny // 2 + 1, 2)),
            dma((ny // 2 + 1, 2)),
            dma((len(back), nq)),
            dma((len(back), nq)),
            dma((7,)),
            dma((7,)),
            dma((len(over_z), nz)),
            dma((len(over_z), nz)),
            dma((nz,)),
            dma((nz,)),
            dma((nz,)),
            dma((nz,)),
            dma((len(back), nq)),
            dma((len(back), nq)),
        ],
        compiler_params=pltpu.CompilerParams(
            collective_id=0, has_side_effects=True, vmem_limit_bytes=62 * 1024 * 1024),
    )(row_adapter.reshape(1, rows), tokens, w_key, jnp.swapaxes(panel_a, 1, 2), up_panels)


def solution(mesh):
    return jax.shard_map(
        functools.partial(local, (X, Y, mesh.shape["tensor"])),
        mesh=mesh,
        in_specs=(
            P("group", "tensor"),
            P("tensor", None),
            P("group", None),
            P("group", "tensor", None),
            P("group", None, None),
        ),
        out_specs=P("tensor", "group"),
        check_vma=False,
    )
```

```python
import functools

import jax
import jax.numpy as jnp
from jax import lax
from jax.experimental import pallas as pl
from jax.experimental.pallas import tpu as pltpu
from jax.sharding import PartitionSpec as P

MESH = pl.DeviceIdType.MESH
F32, BF16 = jnp.float32, jnp.bfloat16
X, Y = 4, 8
CAP = 4

def batches(ny):
    half = ny // 2
    over_z = [[e for d in range(1, half - 1) for e in (d, ny - d)], [0], [half - 1, half + 1], [half]]
    early = [e for d in range(1, half - 1) for e in (d, ny - d)]
    back = ([early] if early else []) + [[half - 1, half + 1], [0, half]]
    return over_z, back


def kernel(dims, ids_hbm, tok_hbm, w_hbm, pa_hbm, up_hbm, out_ref,
           ids_ref, tok, w, panels, ups, place, send, recv, part, zs, zr, rsend, rrecv, rown, srecv, full, widened, lsend, lrecv,
           in_sem, y_ss, y_rs, u_ss, u_rs, x_ss, x_rs, z_ss, z_rs, r_ss, r_rs, s_ss, s_rs, a_ss, a_rs, l_ss, l_rs):
    nx, ny, nz = dims
    nq = 2 * nx
    half = ny // 2
    rows, width = tok.shape
    feat = out_ref.shape[0]
    rk = panels.shape[2]
    slots = 2 * CAP
    over_z, back = batches(ny)
    order = [e for b in over_z for e in b]
    begin, where_back = [], {}
    for b, offs in enumerate(back):
        begin.append(sum(len(o) for o in back[:b]) * nq * slots)
        for i, e in enumerate(offs):
            where_back[e] = (b, i)

    me, t = lax.axis_index("group"), lax.axis_index("tensor")
    mc, my, mx = lax.rem(me, 2), lax.rem(lax.div(me, 2), ny), lax.div(me, 2 * ny)
    mq = mx * 2 + mc

    def along_x(q):
        return {"group": (lax.div(q, 2) * ny + my) * 2 + lax.rem(q, 2)}

    def along_y(step):
        return {"group": (mx * ny + lax.rem(my + step + ny, ny)) * 2 + mc}

    def along_z(p):
        return {"tensor": p}

    def remote(src, dst, ss, rs, where):
        return pltpu.make_async_remote_copy(src, dst, ss, rs, device_id=where, device_id_type=MESH)

    barrier = pltpu.get_barrier_semaphore()
    for step in (-1, 1, ny // 2):
        pl.semaphore_signal(barrier, inc=1, device_id=along_y(step), device_id_type=MESH)

    mine = pl.ds(pl.multiple_of(t * feat, feat), feat)
    loads = [
        pltpu.make_async_copy(pa_hbm, panels.at[0], in_sem.at[0]),
        pltpu.make_async_copy(up_hbm.at[:, :, mine], ups.at[0], in_sem.at[1]),
        pltpu.make_async_copy(tok_hbm, tok, in_sem.at[2]),
        pltpu.make_async_copy(ids_hbm, ids_ref, in_sem.at[4]),
        pltpu.make_async_copy(w_hbm, w, in_sem.at[3]),
    ]
    for c in loads:
        c.start()

    @pl.loop(1, nq)
    def _(j):
        pl.semaphore_signal(barrier, inc=1, device_id=along_x(lax.rem(mq + j, nq)), device_id_type=MESH)

    @pl.loop(1, nz)
    def _(j):
        pl.semaphore_signal(barrier, inc=1, device_id=along_z(lax.rem(t + j, nz)), device_id_type=MESH)

    pl.semaphore_wait(barrier, nq + nz + 1)

    below = [(d, j) for d in range(1, half) for j in (0, 1)] + [(half, 0)]
    above = [(d, 1 - j) for d, j in below]
    steps = len(below)

    def y_copy(n, way):
        d, j = (below if way > 0 else above)[n]
        src, dst = (-(d - 1) * way) % ny, (-d * way) % ny
        return remote(panels.at[src, j], panels.at[dst, j], y_ss.at[n, (1 - way) // 2], y_rs.at[n, (1 - way) // 2],
                      along_y(way))

    def y_step(n):
        for way in (1, -1):
            y_copy(n, way).wait_recv()
            if n + 2 < steps:
                y_copy(n + 2, way).start()

    def u_copy(d, way):
        src, dst = (-(d - 1) * way) % ny, (-d * way) % ny
        return remote(ups.at[src], ups.at[dst], u_ss.at[d, (1 - way) // 2], u_rs.at[d, (1 - way) // 2], along_y(way))

    def u_across():
        return remote(ups.at[0], ups.at[half], u_ss.at[half, 0], u_rs.at[half, 0], along_y(half))

    def u_step(d):
        for way in (1, -1):
            if d > 0:
                u_copy(d, way).wait_recv()
            if d < half - 1:
                u_copy(d + 1, way).start()

    loads[0].wait()
    for n in (0, 1):
        y_copy(n, 1).start()
        y_copy(n, -1).start()
    loads[1].wait()

    loads[3].wait()
    ids = ids_ref[...]
    one_hot = (lax.broadcasted_iota(jnp.int32, (2 * nq * ny, rows), 0) == ids).astype(F32)
    earlier = (lax.broadcasted_iota(jnp.int32, (rows, rows), 0)
               < lax.broadcasted_iota(jnp.int32, (rows, rows), 1)).astype(F32).astype(BF16)
    before = jnp.dot(one_hot.astype(BF16), earlier, preferred_element_type=F32)
    rank = jnp.sum(before * one_hot, axis=0, keepdims=True)
    second, core = lax.rem(ids, 2), lax.rem(lax.div(ids, 2), 2)
    home_y, home_x = lax.rem(lax.div(ids, 4), ny), lax.div(ids, 4 * ny)
    off = lax.rem(home_y - my + ny, ny)
    at = second * CAP
    for e, (b, i) in where_back.items():
        at = at + jnp.where(off == e, begin[b] + i * slots + (home_x * 2 + core) * (len(back[b]) * slots), 0)
    slot = at.astype(F32) + rank
    total = place.shape[0]
    place[...] = (lax.broadcasted_iota(jnp.int32, (total, rows), 0).astype(F32) == slot).astype(F32).astype(BF16)

    loads[2].wait()
    cols = min(256, width)
    for c in range(width // cols):
        send[:, c * cols:(c + 1) * cols] = jnp.dot(
            place[...], tok[:, c * cols:(c + 1) * cols], preferred_element_type=F32).astype(BF16)

    def block(b, q):
        span = len(back[b]) * slots
        return pl.ds(pl.multiple_of(begin[b] + q * span, span), span)

    def x_copy(b, q, at_q):
        return remote(send.at[block(b, q)], recv.at[block(b, at_q)], x_ss.at[b, q], x_rs.at[b, at_q], along_x(q))

    for b in (0, 2, 1):
        @pl.loop(1, nq)
        def _(j):
            x_copy(b, lax.rem(mq + j, nq), mq).start()

        recv[block(b, mq)] = send[block(b, mq)]

    def base_parts():
        loads[4].wait()
        for c in range(nz // 2):
            g = jnp.dot(tok[...], w[:, c * 2 * feat:(c + 1) * 2 * feat], preferred_element_type=F32)
            part[2 * c] = g[:, :feat]
            part[2 * c + 1] = g[:, feat:]

    turn = 1 - 2 * lax.rem(t, 2)

    def at_z(step):
        return lax.rem(t + step * turn + nz, nz)

    def z_copy(n):
        to = (2, -1, 1, -1, 1, 2, -2)[n]
        return remote(zs.at[n], zr.at[n], z_ss.at[n], z_rs.at[n], along_z(at_z(to)))

    def z_send(n, v):
        zs[n] = v.astype(BF16)
        z_copy(n).start()

    def z_first():
        for n, target in enumerate((4, -3, 3, -1, 1)):
            z_send(n, part[at_z(target)])

    def z_second():
        z_copy(0).wait_recv()
        z_copy(1).wait_recv()
        z_send(5, part[at_z(2)] + zr[0].astype(F32) + zr[1].astype(F32))
        z_copy(2).wait_recv()
        z_send(6, part[at_z(-2)] + zr[2].astype(F32))

    top = lax.broadcasted_iota(jnp.int32, (nx, slots, 2 * rk), 1) < CAP
    first = lax.broadcasted_iota(jnp.int32, (nx, slots, 2 * rk), 2) < rk

    def swap(v):
        return jnp.concatenate([v[:, CAP:], v[:, :CAP]], axis=1)

    def x_wait(b):
        @pl.loop(1, nq)
        def _(j):
            q = lax.rem(mq + j, nq)
            x_copy(b, q, q).wait_recv()

    def rank_part(offs):
        b, i = where_back[offs[0]]
        lo = i // 2 * 2 * slots
        span = len(back[b]) * slots
        x = recv[begin[b]:begin[b] + nq * span, :].reshape(nq, span, width)[:, lo:lo + 2 * slots]
        x = x.reshape(nq * 2 * slots, width)
        down = jnp.concatenate([panels[e, j] for e in offs for j in (0, 1)], axis=0)
        r = lax.dot_general(x, down, (((1,), (1,)), ((), ())), preferred_element_type=F32)
        r = r.reshape(nq, 2 * slots, len(offs) * 2 * rk)
        for n, e in enumerate(offs):
            s = where_back[e][1] % 2
            v = r[:, s * slots:(s + 1) * slots, n * 2 * rk:(n + 1) * 2 * rk].reshape(nx, 2, slots, 2 * rk)
            even, odd = v[:, 0], v[:, 1]
            packed = jnp.where(top, jnp.where(first, even, swap(even)), jnp.where(first, swap(odd), odd))
            packed = packed.reshape(nx * slots, 2 * rk)
            rown[order.index(e)] = packed
            rsend[order.index(e)] = packed.astype(BF16)

    def these(b):
        return pl.ds(order.index(over_z[b][0]), len(over_z[b]))

    def rank_copy(b, p, at_p):
        return remote(rsend.at[these(b)], rrecv.at[at_p, these(b)], r_ss.at[b, p], r_rs.at[b, at_p], along_z(p))

    def rank_send(b):
        @pl.loop(1, nz)
        def _(j):
            rank_copy(b, lax.rem(t + j, nz), t).start()

        rrecv[t, these(b)] = jnp.zeros((len(over_z[b]), nx * slots, 2 * rk), BF16)

    share = len(over_z[0]) * nx * slots // nz
    shares = nx * slots // share

    def rows_of(p):
        return lax.div(p, shares), pl.ds(pl.multiple_of(lax.rem(p, shares) * share, share), share)

    def sum_copy(p, at_p):
        return remote(rsend.at[rows_of(p)], srecv.at[at_p], s_ss.at[p], s_rs.at[at_p], along_z(p))

    def full_copy(p, at_p):
        return remote(full.at[at_p], full.at[at_p], a_ss.at[p], a_rs.at[at_p], along_z(p))

    def sum_send():
        @pl.loop(1, nz)
        def _(j):
            sum_copy(lax.rem(t + j, nz), t).start()

        srecv[t] = jnp.zeros((share, 2 * rk), BF16)

    def full_send():
        @pl.loop(1, nz)
        def _(j):
            p = lax.rem(t + j, nz)
            sum_copy(p, p).wait_recv()

        v = rown[rows_of(t)]
        for p in range(nz):
            v = v + srecv[p].astype(F32)
        full[t] = v

        @pl.loop(1, nz)
        def _(j):
            full_copy(lax.rem(t + j, nz), t).start()

    def lora_copy(b, q, at_q):
        return remote(lsend.at[block(b, q)], lrecv.at[block(b, at_q)], l_ss.at[b, q], l_rs.at[b, at_q], along_x(q))

    def widen(b):
        @pl.loop(1, nz)
        def _(j):
            p = lax.rem(t + j, nz)
            (rank_copy(b, p, p) if b else full_copy(p, p)).wait_recv()

        for e in over_z[b]:
            n = order.index(e)
            if b == 0:
                v = full[n * shares:(n + 1) * shares]
            else:
                v = rown[n]
                for p in range(nz):
                    v = v + rrecv[p, n].astype(F32)
            v = v.reshape(nx, slots, 2 * rk)
            zero = jnp.zeros_like(v)
            other = swap(v)
            even = jnp.where(top, jnp.where(first, v, zero), jnp.where(first, zero, other))
            odd = jnp.where(top, jnp.where(first, other, zero), jnp.where(first, zero, v))
            lhs = jnp.concatenate([even[:, None], odd[:, None]], axis=1).reshape(nq * slots, 2 * rk)
            high = lhs.astype(BF16)
            low = (lhs - high.astype(F32)).astype(BF16)
            both = jnp.concatenate([ups[e, j] for j in (0, 1)] * 2, axis=0)
            g = jnp.dot(jnp.concatenate([high, low], axis=1), both, preferred_element_type=F32)
            widened[e] = g.reshape(nq, slots, feat)
        done = [e for o in over_z[:b + 1] for e in o]
        for k, offs in enumerate(back):
            if set(offs) <= set(done) and not set(offs) <= set(done) - set(over_z[b]):
                g = jnp.concatenate([widened[e] for e in offs], axis=1).astype(BF16)
                lsend[begin[k]:begin[k] + nq * len(offs) * slots, :] = g.reshape(nq * len(offs) * slots, feat)

                @pl.loop(1, nq)
                def _(j):
                    lora_copy(k, lax.rem(mq + j, nq), mq).start()

                lrecv[block(k, mq)] = lsend[block(k, mq)]

    def lora_add(b):
        @pl.loop(1, nq)
        def _(j):
            q = lax.rem(mq + j, nq)
            lora_copy(b, q, q).wait_recv()

        lo, n = begin[b], nq * len(back[b]) * slots
        return lax.dot_general(lrecv[lo:lo + n, :], place[lo:lo + n, :], (((0,), (0,)), ((), ())),
                               preferred_element_type=F32)

    last = len(over_z) - 1
    u_at = {2: 0, 4: 1, 6: 2}
    for n in range(steps):
        y_step(n)
        if n in u_at:
            u_step(u_at[n])
        if n == 5:
            u_across().start()
        if n == 0:
            base_parts()
            z_first()
        if n == steps // 2:
            z_second()
        if n == 2:
            x_wait(0)
            rank_part(over_z[0][:2])
        if n == 3:
            rank_part(over_z[0][2:])
            sum_send()
        if n == 4:
            x_wait(2)
            rank_part(over_z[1])
            rank_send(1)
        if n == 5:
            full_send()
            x_wait(1)
            rank_part(over_z[2])
            rank_send(2)
        if n == 6:
            rank_part(over_z[3])
            rank_send(3)
    acc = part[t]
    for n in (3, 4, 5, 6):
        z_copy(n).wait_recv()
        acc = acc + zr[n].astype(F32)
    acc = acc.T
    for b in range(last):
        if b == last - 1:
            for d in range(max(u_at.values()) + 1, half):
                u_step(d)
        widen(b)
    u_across().wait_recv()
    widen(last)
    for b in range(len(back)):
        acc = acc + lora_add(b)
    out_ref[...] = acc.astype(BF16)

    for n in range(steps):
        y_copy(n, 1).wait_send()
        y_copy(n, -1).wait_send()
    for d in range(1, half):
        u_copy(d, 1).wait_send()
        u_copy(d, -1).wait_send()
    u_across().wait_send()
    for n in range(7):
        z_copy(n).wait_send()
    for b in range(len(back)):
        @pl.loop(1, nq)
        def _(j):
            q = lax.rem(mq + j, nq)
            x_copy(b, q, mq).wait_send()
            lora_copy(b, q, mq).wait_send()
    for b in range(1, len(over_z)):
        @pl.loop(1, nz)
        def _(j):
            rank_copy(b, lax.rem(t + j, nz), t).wait_send()

    @pl.loop(1, nz)
    def _(j):
        p = lax.rem(t + j, nz)
        sum_copy(p, t).wait_send()
        full_copy(p, t).wait_send()


def local(dims, tokens, w_key, row_adapter, panel_a, up_panels):
    nx, ny, nz = dims
    rows, width = tokens.shape
    feat = w_key.shape[1] // nz
    rk = panel_a.shape[2]
    nq = 2 * nx
    over_z, back = batches(ny)
    total = ny * nq * 2 * CAP
    vmem = pl.BlockSpec(memory_space=pltpu.VMEM)
    hbm = pl.BlockSpec(memory_space=pl.ANY)
    dma = pltpu.SemaphoreType.DMA
    tiles = (ny, nx * 2 * CAP, 2 * rk)
    share = len(over_z[0]) * nx * 2 * CAP // nz
    return pl.pallas_call(
        functools.partial(kernel, dims),
        out_shape=jax.ShapeDtypeStruct((feat, rows), BF16),
        in_specs=[hbm] * 5,
        out_specs=vmem,
        scratch_shapes=[
            pltpu.VMEM((1, rows), jnp.int32),
            pltpu.VMEM((rows, width), BF16),
            pltpu.VMEM(w_key.shape, BF16),
            pltpu.VMEM((ny, 2, rk, width), BF16),
            pltpu.VMEM((ny, 2, rk, feat), BF16),
            pltpu.VMEM((total, rows), BF16),
            pltpu.VMEM((total, width), BF16),
            pltpu.VMEM((total, width), BF16),
            pltpu.VMEM((nz, rows, feat), F32),
            pltpu.VMEM((7, rows, feat), BF16),
            pltpu.VMEM((7, rows, feat), BF16),
            pltpu.VMEM(tiles, BF16),
            pltpu.VMEM((nz, *tiles), BF16),
            pltpu.VMEM(tiles, F32),
            pltpu.VMEM((nz, share, 2 * rk), BF16),
            pltpu.VMEM((nz, share, 2 * rk), F32),
            pltpu.VMEM((ny, nq, 2 * CAP, feat), F32),
            pltpu.VMEM((total, feat), BF16),
            pltpu.VMEM((total, feat), BF16),
            dma((5,)),
            dma((ny - 1, 2)),
            dma((ny - 1, 2)),
            dma((ny // 2 + 1, 2)),
            dma((ny // 2 + 1, 2)),
            dma((len(back), nq)),
            dma((len(back), nq)),
            dma((7,)),
            dma((7,)),
            dma((len(over_z), nz)),
            dma((len(over_z), nz)),
            dma((nz,)),
            dma((nz,)),
            dma((nz,)),
            dma((nz,)),
            dma((len(back), nq)),
            dma((len(back), nq)),
        ],
        compiler_params=pltpu.CompilerParams(
            collective_id=0, has_side_effects=True, vmem_limit_bytes=62 * 1024 * 1024),
    )(row_adapter.reshape(1, rows), tokens, w_key, jnp.swapaxes(panel_a, 1, 2), up_panels)


def solution(mesh):
    return jax.shard_map(
        functools.partial(local, (X, Y, mesh.shape["tensor"])),
        mesh=mesh,
        in_specs=(
            P("group", "tensor"),
            P("tensor", None),
            P("group", None),
            P("group", "tensor", None),
            P("group", None, None),
        ),
        out_specs=P("tensor", "group"),
        check_vma=False,
    )
```
